32 devices in a mesh: gx: 2 (over y), gy: 4 (over x, core), gz: 4 (over z).
Axes of the slice: x: 2, y: 2, z: 4, core: 2. Of those that a mesh axis runs over, the one named last changes fastest.
Arguments:
- block_state: bfloat16 [2, 64, 10, 32, 1024], P('gx', ('gy', 'gz')), may hold values from -6 to 6
- block_level: int32 [2, 64], P('gx'), may hold values from 0 to 2, as said below
- block_velocity: bfloat16 [2, 64, 3], P('gx', ('gy', 'gz')), may hold values from -1 to 1
- diffusivity: float32 [10], replicated, may hold values from 0.05 to 0.6
- reaction_matrix: float32 [10, 10], replicated, may hold values from -3 to 3
- ghost_source: int32 [2, 64, 6], P('gx'), may hold values from 0 to 63, as said below
- swap_bit: int32 [2, 4, 4], P('gx', 'gy', 'gz'), may hold values from -1 to 0, as said below
- swap_slot: int32 [2, 4, 4], P('gx', 'gy', 'gz'), may hold values from 0 to 3, as said below
Outputs:
- new_state: bfloat16 [2, 64, 10, 32, 1024], P('gx', ('gy', 'gz'))
The draws below stay inside these ranges and needn't reach their ends.
Inputs may be any that keep to these rules, and one draw needn't show every extreme that they name: `block_level`: levels are 0, 1 or 2; all blocks of some devices have level 2. `ghost_source`: ghost sources lie in the same gx slab; blocks of a slab are numbered device by device in gy+gz order, 4 a device. Among the 24 ghost faces of the blocks of one device, at most 2 come from the blocks of any one device, and exactly 2 from some device. `swap_bit`: all devices of one (gy, gz) column share the value, so trade partners are paired; -1 means that the column trades no block. `swap_slot`: of two partners, the one whose sum of 2 ** level over its blocks is larger (ties: the lower gx index) names its first block of highest level, the other its first block of lowest level.
All inputs are finite; a program needn't handle non-finite values.
Results may differ from the reference program's by a relative error of at most 0.001.
Values may be sent and summed in bfloat16 or wider, within the bound.
A program may use at most 128 MiB of HBM per device.

```python
import math
import jax
import jax.numpy as jnp
from jax import lax

F = 10
B = 32
NB = 4
SLAB_BLOCKS = 64
CAP = 2
N_GX = 2
N_GY = 4
N_GZ = 4


def level_table(key):
    slab = N_GY * N_GZ
    bit_total = N_GX.bit_length() - 1
    top = 1 << bit_total - 1
    heated = jax.random.randint(jax.random.fold_in(key, 101), (N_GX, slab, 1), 0, 4) == 0
    lower = jax.random.randint(jax.random.fold_in(key, 102), (N_GX, slab, NB), 0, 2)
    table = jnp.where(heated, 2, lower).astype(jnp.int32)
    slab_ids = jnp.arange(N_GX, dtype=jnp.int32)[:, None, None]
    column = jnp.arange(slab, dtype=jnp.int32)[None, :, None]
    within = jnp.arange(NB, dtype=jnp.int32)[None, None, :]
    low_group = jnp.bitwise_and(slab_ids, top) == 0
    pattern = jnp.where(low_group & (within == NB - 1), 2, 0).astype(jnp.int32)
    table = jnp.where(column == 0, pattern, table)
    table = jnp.where(column == 1, jnp.int32(2), table)
    return table.astype(jnp.int32)


def bit_table(key):
    bit_total = N_GX.bit_length() - 1
    slab = N_GY * N_GZ
    column = jax.random.randint(jax.random.fold_in(key, 103), (slab,), -1, bit_total)
    column = column.at[0].set(bit_total - 1).at[1].set(-1)
    column = column.reshape(1, N_GY, N_GZ)
    return jnp.broadcast_to(column, (N_GX, N_GY, N_GZ)).astype(jnp.int32)


def draw_block_level(key, part):
    return level_table(key).reshape(N_GX, N_GY * N_GZ * NB)


def draw_swap_bit(key, part):
    return bit_table(key)


def draw_swap_slot(key, part):
    slab = N_GY * N_GZ
    levels = level_table(key)
    bits = bit_table(key).reshape(N_GX, slab)
    loads = jnp.sum(jnp.left_shift(jnp.int32(1), levels), axis=2)
    slab_ids = jnp.arange(N_GX, dtype=jnp.int32)[:, None]
    flips = jnp.where(bits < 0, jnp.int32(0), jnp.left_shift(jnp.int32(1), jnp.maximum(bits, 0)))
    partner = jnp.bitwise_xor(slab_ids, flips)
    other = jnp.take_along_axis(loads, partner, axis=0)
    heavier = (loads > other) | (loads == other) & (slab_ids < partner)
    chosen = jnp.where(heavier, jnp.argmax(levels, axis=2), jnp.argmin(levels, axis=2))
    return chosen.astype(jnp.int32).reshape(N_GX, N_GY, N_GZ)


def draw_ghost_source(key, part):
    slab = N_GY * N_GZ
    requests = 6 * NB
    limit = CAP
    keys = jax.random.split(jax.random.fold_in(key, 104), N_GX * slab)

    def one_device(subkey):
        first_key, order_key, shuffle_key, slot_key = jax.random.split(subkey, 4)
        first = jax.random.randint(first_key, (), 0, slab)
        owners = jnp.arange(slab * limit, dtype=jnp.int32) // limit
        scores = jax.random.permutation(order_key, slab * limit).astype(jnp.int32)
        scores = scores + jnp.where(owners == first, slab * limit, 0)
        ordering = jnp.argsort(scores, stable=True)
        others = owners[ordering][:requests - limit]
        devices = jnp.concatenate([jnp.full((limit,), first, jnp.int32), others])
        devices = devices[jax.random.permutation(shuffle_key, requests)]
        slots = jax.random.randint(slot_key, (requests,), 0, NB)
        return devices * NB + slots
    table = jax.vmap(one_device)(keys)
    return table.reshape(N_GX, slab * NB, 6).astype(jnp.int32)


def steps_of(rng, shape, pieces, smallest, top_value):
    def one(axis_at, shards_of):
        steps = jax.random.uniform(jax.random.fold_in(jax.random.fold_in(rng, 6), axis_at), (shards_of,), jnp.float32, smallest / len(pieces), top_value / len(pieces))
        return jnp.repeat(jnp.exp(steps), shape[axis_at] // shards_of).reshape((-1,) + (1,) * (len(shape) - axis_at - 1))

    level = one(*pieces[0])
    for cut in pieces[1:]:
        level = level * one(*cut)
    return level


def normal_values(stream_key, shape, scale, most, shards=(), kind=jnp.bfloat16):
    level = steps_of(stream_key, shape, shards, -0.22, 0.18) if shards else 1.0
    entries = jax.random.normal(stream_key, shape, jnp.float32) * scale * level
    return jnp.minimum(jnp.maximum(entries, -most), most).astype(kind)


def setup_inputs(seed: int = 0) -> dict:
    arg_keys = jax.random.split(jax.random.key(seed), 9)
    block_state = normal_values(arg_keys[0], (N_GX, SLAB_BLOCKS, F, B, B * B), 1.0, 6.0, ((0, 2), (1, 16)))
    block_level = draw_block_level(jax.random.fold_in(arg_keys[8], 71), 0)
    block_velocity = jnp.clip(jax.random.uniform(arg_keys[2], (N_GX, SLAB_BLOCKS, 3), jnp.float32, -1.0, 1.0) * steps_of(arg_keys[2], (N_GX, SLAB_BLOCKS, 3), ((0, 2), (1, 16)), -0.4, 0.0), -1.0, 1.0).astype(jnp.bfloat16)
    diffusivity = jnp.clip(jnp.exp(jax.random.uniform(arg_keys[3], (F,), jnp.float32, math.log(0.05), math.log(0.6))), 0.05, 0.6)
    reaction_matrix = normal_values(arg_keys[4], (F, F), 0.5, 3.0, (), jnp.float32)
    ghost_source = draw_ghost_source(jax.random.fold_in(arg_keys[8], 71), 0)
    swap_bit = draw_swap_bit(jax.random.fold_in(arg_keys[8], 71), 0)
    swap_slot = draw_swap_slot(jax.random.fold_in(arg_keys[8], 71), 0)
    return dict(block_state=block_state, block_level=block_level, block_velocity=block_velocity, diffusivity=diffusivity, reaction_matrix=reaction_matrix, ghost_source=ghost_source, swap_bit=swap_bit, swap_slot=swap_slot)


dt_base = 0.05


def face_layer(donor, face_no):
    layers = [donor[:, 0], donor[:, -1], donor[:, :, 0], donor[:, :, -1], donor[:, :, :, 0], donor[:, :, :, -1]]
    return layers[face_no]


def coarsen_face(layer):
    fields, rows, cols = layer.shape
    means = jnp.mean(layer.reshape(fields, rows // 2, 2, cols // 2, 2), axis=(2, 4))
    return jnp.repeat(jnp.repeat(means, 2, axis=1), 2, axis=2)


def upwind_term(values, minus, plus, speed):
    return jnp.maximum(speed, 0.0) * (values - minus) + jnp.minimum(speed, 0.0) * (plus - values)


def advance(species_field, layers, own_level, velocity, diffusivity, reaction_matrix):
    substeps = jnp.left_shift(jnp.int32(1), own_level)
    scale = substeps.astype(jnp.float32)
    step_size = dt_base / scale
    rates = diffusivity[:, None, None, None]

    def substep(index, values):
        minus_x = jnp.concatenate([layers[0][:, None], values[:, :-1]], axis=1)
        plus_x = jnp.concatenate([values[:, 1:], layers[1][:, None]], axis=1)
        minus_y = jnp.concatenate([layers[2][:, :, None], values[:, :, :-1]], axis=2)
        plus_y = jnp.concatenate([values[:, :, 1:], layers[3][:, :, None]], axis=2)
        negative_depth_face = jnp.concatenate([layers[4][..., None], values[..., :-1]], axis=3)
        plus_z = jnp.concatenate([values[..., 1:], layers[5][..., None]], axis=3)
        diffused_field = (minus_x + plus_x) + (minus_y + plus_y) + (negative_depth_face + plus_z) - 6.0 * values
        upwind = (upwind_term(values, minus_x, plus_x, velocity[0])
                  + upwind_term(values, minus_y, plus_y, velocity[1])
                  + upwind_term(values, negative_depth_face, plus_z, velocity[2]))
        sender_rank = jnp.einsum("fg,gxyz->fxyz", reaction_matrix, values, precision=lax.Precision.HIGHEST)
        change = rates * diffused_field * (scale * scale) - upwind * scale + sender_rank
        return values + step_size * change

    return lax.fori_loop(jnp.int32(0), substeps, substep, species_field)


def reference(block_state, block_level, block_velocity, diffusivity, reaction_matrix, ghost_source, swap_bit, swap_slot):
    slab = N_GY * N_GZ
    total = N_GX * SLAB_BLOCKS

    def per_block(index):
        slab_no = index // SLAB_BLOCKS
        row_no = index % SLAB_BLOCKS
        species_field = block_state[slab_no, row_no].astype(jnp.float32).reshape(F, B, B, B)
        own_level = block_level[slab_no, row_no]
        layers = []
        for face_no in range(6):
            sender_rank = ghost_source[slab_no, row_no, face_no]
            donor = block_state[slab_no, sender_rank].astype(jnp.float32).reshape(F, B, B, B)
            layer = face_layer(donor, face_no ^ 1)
            layers.append(jnp.where(block_level[slab_no, sender_rank] != own_level, coarsen_face(layer), layer))
        velocity = block_velocity[slab_no, row_no].astype(jnp.float32)
        result = advance(species_field, layers, own_level, velocity, diffusivity, reaction_matrix)
        return result.astype(jnp.bfloat16).reshape(F, B, B * B)

    fresh = lax.map(per_block, jnp.arange(total, dtype=jnp.int32)).reshape(N_GX, SLAB_BLOCKS, F, B, B * B)
    bits = swap_bit.reshape(N_GX, slab).astype(jnp.int32)
    slots = swap_slot.reshape(N_GX, slab).astype(jnp.int32)
    slab_ids = jnp.arange(N_GX, dtype=jnp.int32)[:, None]
    column = jnp.arange(slab, dtype=jnp.int32)[None, :]
    flips = jnp.where(bits < 0, jnp.int32(0), jnp.left_shift(jnp.int32(1), jnp.maximum(bits, 0)))
    partner = jnp.bitwise_xor(slab_ids, flips)
    partner_slot = slots[partner, column]
    within = jnp.arange(NB, dtype=jnp.int32)[None, None, :]
    traded = within == slots[:, :, None]
    from_slab = jnp.where(traded, partner[:, :, None], slab_ids[:, :, None])
    from_row = column[:, :, None] * NB + jnp.where(traded, partner_slot[:, :, None], within)
    return fresh[from_slab.reshape(N_GX, SLAB_BLOCKS), from_row.reshape(N_GX, SLAB_BLOCKS)]
```

```python
import functools

import jax
import jax.numpy as jnp
from jax import lax
from jax.experimental import pallas as pl
from jax.experimental.pallas import tpu as pltpu
from jax.sharding import PartitionSpec as P

dt_base = 0.05
GROUP = 4
VMEM_LIMIT = 56 * 1024 * 1024


def swapped(x, axis, bit):
    return lax.ppermute(x, axis, [(i, i ^ 1 << bit) for i in range(lax.axis_size(axis))])


def lane_iota():
    return lax.broadcasted_iota(jnp.int32, (8, 128), 1)


def row_iota():
    return lax.broadcasted_iota(jnp.int32, (8, 128), 0)


def spread_rows(x_ref, f, rows_ref):
    for half in range(2):
        for t in range(8):
            v = x_ref[f, 16 * half : 16 * half + 16, 128 * t : 128 * t + 128].astype(jnp.float32)
            at = (2 * half * 8 + t) * 8
            rows_ref[at : at + 8, :] = v[:8]
            rows_ref[at + 64 : at + 72, :] = v[8:]


def plane_rows(i):
    return pl.ds((i // 8) * 64 + i % 8, 8, stride=8)


def pack_kernel(sel_ref, x_ref, out_ref, faces, rows):
    step = pl.program_id(0)
    lane = lane_iota()
    k = lane % 32

    def pair(fp, carry):
        got = [[], [], [], [], [], []]
        for half in range(2):
            f = fp * 2 + half
            spread_rows(x_ref.at[0], f, rows)
            low_z = jnp.zeros((8, 128), jnp.float32)
            high_z = jnp.zeros((8, 128), jnp.float32)
            for i in range(32):
                plane = rows[plane_rows(i), :]
                if i == 0:
                    got[0].append(plane)
                if i == 31:
                    got[1].append(plane)
                here = k == i
                low_z = jnp.where(here, pltpu.roll(plane, i, 1) if i else plane, low_z)
                high_z = jnp.where(
                    here, pltpu.roll(plane, (i + 97) % 128, 1) if i != 31 else plane, high_z
                )
            low_y = rows[0:8, :]
            high_y = rows[56:64, :]
            for it in range(1, 4):
                here = lane // 32 == it
                low_y = jnp.where(
                    here, pltpu.roll(rows[it * 64 : it * 64 + 8, :], 32 * it, 1), low_y
                )
            high_y = pltpu.roll(high_y, 32, 1)
            for it in range(1, 4):
                here = lane // 32 == it
                v = rows[it * 64 + 56 : it * 64 + 64, :]
                high_y = jnp.where(
                    here, pltpu.roll(v, (32 * it + 32) % 128, 1) if it != 3 else v, high_y
                )
            got[2].append(low_y)
            got[3].append(high_y)
            got[4].append(low_z)
            got[5].append(high_z)
        at = pl.multiple_of(fp * 16, 16)
        for face in range(6):
            both = jnp.concatenate(got[face], axis=0).astype(jnp.bfloat16)
            faces[step * 6 + face, pl.ds(at, 16), :] = both
        return carry

    lax.fori_loop(0, x_ref.shape[1] // 2, pair, 0)

    @pl.when(step == pl.num_programs(0) - 1)
    def _():
        def place(n, carry):
            out_ref[n] = faces[sel_ref[n]]
            return carry

        lax.fori_loop(0, out_ref.shape[0], place, 0)


def pack_faces(blocks, sel):
    per_dev, fields, cells, plane = blocks.shape
    return pl.pallas_call(
        pack_kernel,
        grid_spec=pltpu.PrefetchScalarGridSpec(
            num_scalar_prefetch=1,
            grid=(per_dev,),
            in_specs=[pl.BlockSpec((1, fields, cells, plane), lambda g, *_: (g, 0, 0, 0))],
            out_specs=pl.BlockSpec((sel.shape[0], fields * 8, 128), lambda g, *_: (0, 0, 0)),
            scratch_shapes=[
                pltpu.VMEM((per_dev * 6, fields * 8, 128), jnp.bfloat16),
                pltpu.VMEM((256, 128), jnp.float32),
            ],
        ),
        out_shape=jax.ShapeDtypeStruct((sel.shape[0], fields * 8, 128), jnp.bfloat16),
        compiler_params=pltpu.CompilerParams(vmem_limit_bytes=VMEM_LIMIT),
    )(sel, blocks)


def pair_sum(x, distance, axis, bit_clear):
    size = x.shape[axis]
    other = jnp.where(
        bit_clear, pltpu.roll(x, size - distance, axis), pltpu.roll(x, distance, axis)
    )
    return x + other


def advance_kernel(
    ids_ref, levels_ref, sources_ref, base_ref, speed_ref, rate_ref, react_ref,
    x_ref, faces_ref, o_ref,
    u, ghost, layers, coef, rows,
):
    fields = x_ref.shape[1]
    per_dev = speed_ref.shape[0] // 3
    block = ids_ref[pl.program_id(0)]
    base = base_ref[0]
    own_level = levels_ref[base + block]
    substeps = jnp.left_shift(jnp.int32(1), own_level)
    scale = substeps.astype(jnp.float32)
    dt = jnp.where(own_level == 0, dt_base, jnp.where(own_level == 1, dt_base / 2, dt_base / 4))
    lane, row = lane_iota(), row_iota()
    k = lane % 32
    at_low_z, at_high_z = k == 0, k == 31
    at_low_y = (row == 0) & (lane < 32)
    at_high_y = (row == 7) & (lane >= 96)

    for face in range(6):
        request = block * 6 + face
        donor = sources_ref[base * 6 + request]
        dev = donor // per_dev

        def same(r, found):
            hit = (sources_ref[base * 6 + r] // per_dev == dev) & (r < request)
            return jnp.where(hit, 1, found)

        second = lax.fori_loop(0, per_dev * 6, same, jnp.int32(0))
        layers[face] = faces_ref[dev * 2 + second].astype(jnp.float32)

        @pl.when(levels_ref[donor] != own_level)
        def _():
            def coarsen(f, carry):
                at = pl.ds(pl.multiple_of(f * 8, 8), 8)
                v = pair_sum(layers[face, at, :], 1, 1, lane % 2 == 0)
                if face in (2, 3):
                    v = pair_sum(v, 1, 0, row % 2 == 0)
                else:
                    v = pair_sum(v, 32, 1, lane // 32 % 2 == 0)
                layers[face, at, :] = v * 0.25
                return carry

            lax.fori_loop(0, fields, coarsen, 0)

    speeds = [speed_ref[block * 3 + d] for d in range(3)]
    minus = [jnp.maximum(v, 0.0) * scale * dt for v in speeds]
    plus = [-jnp.minimum(v, 0.0) * scale * dt for v in speeds]
    outflow = minus[0] + plus[0] + minus[1] + plus[1] + minus[2] + plus[2]

    def prepare(f, carry):
        rate = rate_ref[f] * (scale * scale) * dt
        coef[f, 0] = jnp.full((8, 128), rate + minus[0])
        coef[f, 1] = jnp.full((8, 128), rate + plus[0])
        coef[f, 2] = jnp.where(at_low_y, 0.0, rate + minus[1])
        coef[f, 3] = jnp.where(at_high_y, 0.0, rate + plus[1])
        coef[f, 4] = jnp.where(at_low_z, 0.0, rate + minus[2])
        coef[f, 5] = jnp.where(at_high_z, 0.0, rate + plus[2])
        for e in range(fields):
            own = jnp.where(f == e, 1.0 - 6.0 * rate - outflow, 0.0)
            coef[f, 6 + e] = jnp.full((8, 128), dt * react_ref[f * fields + e] + own)

        at = pl.ds(pl.multiple_of(f * 8, 8), 8)
        for side in range(2):
            u[side, f, 0] = layers[0, at, :]
            u[side, f, 33] = layers[1, at, :]
        low_y = layers[2, at, :] * (rate + minus[1])
        high_y = layers[3, at, :] * (rate + plus[1])
        low_z = layers[4, at, :] * (rate + minus[2])
        high_z = layers[5, at, :] * (rate + plus[2])
        for it in range(4):
            low_y_it = jnp.where(
                lane < 32, pltpu.roll(low_y, (128 - 32 * it) % 128, 1) if it else low_y, 0.0
            )
            high_y_it = jnp.where(
                lane >= 96, pltpu.roll(high_y, 96 - 32 * it, 1) if it != 3 else high_y, 0.0
            )
            for s in range(8):
                i = it * 8 + s
                v = jnp.where(at_low_z, pltpu.roll(low_z, 128 - i, 1) if i else low_z, 0.0)
                v = jnp.where(at_high_z, pltpu.roll(high_z, 31 - i, 1) if i != 31 else high_z, v)
                low = pltpu.roll(low_y_it, 8 - s, 0) if s else low_y_it
                high = pltpu.roll(high_y_it, 7 - s, 0) if s != 7 else high_y_it
                ends = jnp.where(row == 0, low, jnp.where(row == 7, high, 0.0))
                ghost[f, i] = v + ends
        spread_rows(x_ref.at[0], f, rows)
        for i in range(32):
            u[0, f, i + 1] = rows[plane_rows(i), :]
        return carry

    lax.fori_loop(0, fields, prepare, 0)

    def substep(index, carry):
        now = index % 2
        later = 1 - now

        def planes(g, inner):
            first = g * GROUP
            mid = [[u[now, f, first + 1 + p] for p in range(GROUP)] for f in range(fields)]
            for f in range(fields):
                before = [u[now, f, first]] + mid[f][:-1]
                after = mid[f][1:] + [u[now, f, first + GROUP + 1]]
                total = []
                for p in range(GROUP):
                    c = mid[f][p]
                    left = pltpu.roll(c, 32, 1)
                    minus_y = jnp.where(lane < 32, pltpu.roll(left, 1, 0), left)
                    right = pltpu.roll(c, 96, 1)
                    plus_y = jnp.where(lane >= 96, pltpu.roll(right, 7, 0), right)
                    v = ghost[f, first + p] + coef[f, 0] * before[p]
                    v = v + coef[f, 1] * after[p]
                    v = v + coef[f, 2] * minus_y
                    v = v + coef[f, 3] * plus_y
                    v = v + coef[f, 4] * pltpu.roll(c, 1, 1)
                    v = v + coef[f, 5] * pltpu.roll(c, 127, 1)
                    total.append(v)
                for e in range(fields):
                    weight = coef[f, 6 + e]
                    for p in range(GROUP):
                        total[p] = total[p] + weight * mid[e][p]
                for p in range(GROUP):
                    u[later, f, first + 1 + p] = total[p]
            return inner

        lax.fori_loop(0, 32 // GROUP, planes, 0)
        return carry

    lax.fori_loop(0, substeps, substep, 0)
    last = substeps % 2

    def finish(f, carry):
        for i in range(32):
            rows[plane_rows(i), :] = u[last, f, i + 1]
        for half in range(2):
            for t in range(8):
                at = (2 * half * 8 + t) * 8
                both = jnp.concatenate([rows[at : at + 8, :], rows[at + 64 : at + 72, :]], axis=0)
                o_ref[0, f, 16 * half : 16 * half + 16, 128 * t : 128 * t + 128] = both.astype(
                    jnp.bfloat16
                )
        return carry

    lax.fori_loop(0, fields, finish, 0)


def advance(blocks, faces, ids, scalars, out_blocks):
    per_dev, fields, cells, plane = blocks.shape
    count = ids.shape[0]
    block_shape = (1, fields, cells, plane)
    picked = lambda g, ids, *_: (ids[g], 0, 0, 0)
    return pl.pallas_call(
        advance_kernel,
        grid_spec=pltpu.PrefetchScalarGridSpec(
            num_scalar_prefetch=7,
            grid=(count,),
            in_specs=[
                pl.BlockSpec(block_shape, picked),
                pl.BlockSpec(faces.shape, lambda g, *_: (0, 0, 0)),
            ],
            out_specs=pl.BlockSpec(
                block_shape, picked if out_blocks > 1 else lambda g, *_: (0, 0, 0, 0)
            ),
            scratch_shapes=[
                pltpu.VMEM((2, fields, cells + 2, 8, 128), jnp.float32),
                pltpu.VMEM((fields, cells, 8, 128), jnp.float32),
                pltpu.VMEM((6, fields * 8, 128), jnp.float32),
                pltpu.VMEM((fields, 6 + fields, 8, 128), jnp.float32),
                pltpu.VMEM((256, 128), jnp.float32),
            ],
        ),
        out_shape=jax.ShapeDtypeStruct((out_blocks, fields, cells, plane), jnp.bfloat16),
        compiler_params=pltpu.CompilerParams(vmem_limit_bytes=VMEM_LIMIT),
        cost_estimate=pl.CostEstimate(
            flops=count * 40_000_000_000, bytes_accessed=count * 1_400_000, transcendentals=0
        ),
    )(ids, *scalars, blocks, faces)


def local(
    block_state,
    block_level,
    block_velocity,
    diffusivity,
    reaction_matrix,
    ghost_source,
    swap_bit,
    swap_slot,
):
    blocks = block_state[0]
    per_dev = blocks.shape[0]
    requests = per_dev * 6
    peers = lax.axis_size(("gy", "gz"))
    my_index = lax.axis_index(("gy", "gz"))
    base = my_index * per_dev
    wanted = ghost_source[0].reshape(peers, requests)
    order = jnp.arange(requests, dtype=jnp.int32)[None, :]
    code = order * 64 + wanted % per_dev * 6 + (order % 6 ^ 1)
    match = wanted // per_dev == my_index
    first = jnp.min(jnp.where(match, code, requests * 64), axis=1)
    final = jnp.max(jnp.where(match, code, 0), axis=1)
    sel = jnp.stack([first, final], axis=1).reshape(2 * peers) % 64

    outgoing = pack_faces(blocks, sel)
    arrived = lax.all_to_all(outgoing, ("gy", "gz"), split_axis=0, concat_axis=0, tiled=True)

    slot_here = swap_slot[0, 0, 0]
    bit_here = swap_bit[0, 0, 0]
    others = jnp.arange(per_dev - 1, dtype=jnp.int32)
    others = others + (others >= slot_here).astype(jnp.int32)
    scalars = (
        block_level[0],
        ghost_source[0].reshape(-1),
        base.astype(jnp.int32)[None],
        block_velocity[0].astype(jnp.float32).reshape(-1),
        diffusivity,
        reaction_matrix.reshape(-1),
    )
    departing = advance(blocks, arrived, slot_here[None], scalars, 1)
    bit_count = lax.axis_size("gx").bit_length() - 1
    partners = [swapped(departing, "gx", bit_no) for bit_no in range(bit_count)]
    rest = advance(blocks, arrived, others, scalars, per_dev)
    coming = departing
    for bit_no in range(bit_count):
        coming = jnp.where(bit_here == bit_no, partners[bit_no], coming)
    result = lax.dynamic_update_index_in_dim(rest, coming[0], slot_here, 0)
    return result[None]


def solution(mesh):
    in_specs = (
        P("gx", ("gy", "gz"), None, None, None),
        P("gx", None),
        P("gx", ("gy", "gz"), None),
        P(),
        P(),
        P("gx", None, None),
        P("gx", "gy", "gz"),
        P("gx", "gy", "gz"),
    )
    out_specs = P("gx", ("gy", "gz"), None, None, None)
    return jax.shard_map(local, mesh=mesh, in_specs=in_specs, out_specs=out_specs, check_vma=False)
```

```python
import functools

import jax
import jax.numpy as jnp
from jax import lax
from jax.experimental import pallas as pl
from jax.experimental.pallas import tpu as pltpu
from jax.sharding import PartitionSpec as P

dt_base = 0.05
VMEM_LIMIT = 56 * 1024 * 1024


def swapped(x, axis, bit):
    return lax.ppermute(x, axis, [(i, i ^ 1 << bit) for i in range(lax.axis_size(axis))])


def lane_iota():
    return lax.broadcasted_iota(jnp.int32, (8, 128), 1)


def row_iota():
    return lax.broadcasted_iota(jnp.int32, (8, 128), 0)


def regroup_matrix():
    r = lax.broadcasted_iota(jnp.int32, (512, 512), 0)
    c = lax.broadcasted_iota(jnp.int32, (512, 512), 1)
    target = (r // 32) % 4 * 128 + r // 128 * 32 + r % 32
    return jnp.where(c == target, 1.0, 0.0).astype(jnp.bfloat16)


def regroup_in(x_ref, matrix, rows):
    fields = x_ref.shape[1]
    height = fields * 32
    for half in range(2):
        tiles = [
            x_ref[0, :, :, 128 * (half + 2 * m) : 128 * (half + 2 * m) + 128].reshape(height, 128)
            for m in range(4)
        ]
        moved = jnp.dot(
            jnp.concatenate(tiles, axis=1), matrix[...], preferred_element_type=jnp.float32
        )
        for g in range(4):
            at = (half * 4 + g) * height
            rows[at : at + height, :] = moved[:, 128 * g : 128 * g + 128]


def plane_rows(fields, f, ii, jj):
    return pl.ds(jj * fields * 32 + f * 32 + ii, 8, stride=4)


def pack_kernel(sel_ref, x_ref, out_ref, faces, rows, matrix):
    step = pl.program_id(0)
    fields = x_ref.shape[1]
    lane = lane_iota()
    k = lane % 32

    @pl.when(step == 0)
    def _():
        matrix[...] = regroup_matrix()

    regroup_in(x_ref, matrix, rows)

    def pair(fp, carry):
        got = [[], [], [], [], [], []]
        for half in range(2):
            f = fp * 2 + half
            got[0].append(rows[pl.ds(f * 32, 8, stride=fields * 32), :])
            got[1].append(rows[pl.ds(f * 32 + 31, 8, stride=fields * 32), :])
            low_y = high_y = low_z = high_z = jnp.zeros((8, 128), jnp.float32)
            for ii in range(4):
                for jj in range(8):
                    plane = rows[plane_rows(fields, f, ii, jj), :]
                    n = ii * 8 + jj
                    here = k == n
                    low_z = jnp.where(here, pltpu.roll(plane, n, 1) if n else plane, low_z)
                    high_z = jnp.where(
                        here, pltpu.roll(plane, n + 97, 1) if n != 31 else plane, high_z
                    )
                    here = lane // 32 == ii
                    if jj == 0:
                        low_y = jnp.where(here, pltpu.roll(plane, 32 * ii, 1) if ii else plane, low_y)
                    if jj == 7:
                        moved = pltpu.roll(plane, 32 * ii + 32, 1) if ii != 3 else plane
                        high_y = jnp.where(here, moved, high_y)
            got[2].append(low_y)
            got[3].append(high_y)
            got[4].append(low_z)
            got[5].append(high_z)
        at = pl.multiple_of(fp * 16, 16)
        for face in range(6):
            both = jnp.concatenate(got[face], axis=0).astype(jnp.bfloat16)
            faces[step * 6 + face, pl.ds(at, 16), :] = both
        return carry

    lax.fori_loop(0, fields // 2, pair, 0)

    @pl.when(step == pl.num_programs(0) - 1)
    def _():
        def place(n, carry):
            out_ref[n] = faces[sel_ref[n]]
            return carry

        lax.fori_loop(0, out_ref.shape[0], place, 0, unroll=4)


def pack_faces(blocks, sel):
    per_dev, fields, cells, plane = blocks.shape
    return pl.pallas_call(
        pack_kernel,
        grid_spec=pltpu.PrefetchScalarGridSpec(
            num_scalar_prefetch=1,
            grid=(per_dev,),
            in_specs=[pl.BlockSpec((1, fields, cells, plane), lambda g, *_: (g, 0, 0, 0))],
            out_specs=pl.BlockSpec((sel.shape[0], fields * 8, 128), lambda g, *_: (0, 0, 0)),
            scratch_shapes=[
                pltpu.VMEM((per_dev * 6, fields * 8, 128), jnp.bfloat16),
                pltpu.VMEM((fields * 256, 128), jnp.float32),
                pltpu.VMEM((512, 512), jnp.bfloat16),
            ],
        ),
        out_shape=jax.ShapeDtypeStruct((sel.shape[0], fields * 8, 128), jnp.bfloat16),
        compiler_params=pltpu.CompilerParams(vmem_limit_bytes=VMEM_LIMIT),
    )(sel, blocks)


def pair_sum(x, distance, axis, bit_clear):
    size = x.shape[axis]
    other = jnp.where(
        bit_clear, pltpu.roll(x, size - distance, axis), pltpu.roll(x, distance, axis)
    )
    return x + other


def advance_kernel(
    meta_ref, speed_ref, rate_ref, react_ref,
    x_ref, faces_ref, o_ref,
    u, ghost, layers, ends, coef, rows, matrix,
):
    fields = x_ref.shape[1]
    step = pl.program_id(0)
    count = pl.num_programs(0)
    per_dev = speed_ref.shape[0] // 3
    requests = per_dev * 6
    block = meta_ref[step]
    own_level = meta_ref[per_dev + block]
    substeps = jnp.left_shift(jnp.int32(1), own_level)
    scale = substeps.astype(jnp.float32)
    dt = jnp.where(own_level == 0, dt_base, jnp.where(own_level == 1, dt_base / 2, dt_base / 4))
    lane, row = lane_iota(), row_iota()
    k = lane % 32
    at_low_z, at_high_z = k == 0, k == 31

    @pl.when(step == 0)
    def _():
        matrix[...] = regroup_matrix()

    regroup_in(x_ref, matrix, rows)

    tall_lane = lax.broadcasted_iota(jnp.int32, (fields * 8, 128), 1)
    tall_row = lax.broadcasted_iota(jnp.int32, (fields * 8, 128), 0)
    for face in range(6):
        request = block * 6 + face
        layers[face] = faces_ref[meta_ref[2 * per_dev + request]].astype(jnp.float32)

        @pl.when(meta_ref[2 * per_dev + requests + request] > 0)
        def _():
            v = pair_sum(layers[face], 1, 1, tall_lane % 2 == 0)
            if face < 2:
                v = pair_sum(v, 1, 0, tall_row % 2 == 0)
            elif face < 4:
                v = pair_sum(v, 32, 1, tall_lane // 32 % 2 == 0)
            else:
                v = pair_sum(v, 8, 1, tall_lane // 8 % 2 == 0)
            layers[face] = v * 0.25

    speeds = [speed_ref[block * 3 + d] for d in range(3)]
    minus = [jnp.maximum(v, 0.0) * scale * dt for v in speeds]
    plus = [-jnp.minimum(v, 0.0) * scale * dt for v in speeds]
    outflow = minus[0] + plus[0] + minus[1] + plus[1] + minus[2] + plus[2]

    def halo_low_x(plane, f, jj):
        edge = layers[0, pl.ds(f * 8 + jj, 1), :]
        return jnp.where(row == 0, edge, pltpu.roll(plane, 1, 0))

    def halo_high_x(plane, f, jj):
        edge = layers[1, pl.ds(f * 8 + jj, 1), :]
        return jnp.where(row == 7, edge, pltpu.roll(plane, 7, 0))

    def halo_low_y(plane, f, ii):
        return jnp.where(lane < 32, ends[0, f, ii], pltpu.roll(plane, 32, 1))

    def halo_high_y(plane, f, ii):
        return jnp.where(lane >= 96, ends[1, f, ii], pltpu.roll(plane, 96, 1))

    def prepare(f, carry):
        rate = rate_ref[f] * (scale * scale) * dt
        coef[f, 0] = jnp.full((8, 128), rate + minus[0])
        coef[f, 1] = jnp.full((8, 128), rate + plus[0])
        coef[f, 2] = jnp.full((8, 128), rate + minus[1])
        coef[f, 3] = jnp.full((8, 128), rate + plus[1])
        coef[f, 4] = jnp.where(at_low_z, 0.0, rate + minus[2])
        coef[f, 5] = jnp.where(at_high_z, 0.0, rate + plus[2])
        for e in range(fields):
            own = jnp.where(f == e, 1.0 - 6.0 * rate - outflow, 0.0)
            coef[f, 6 + e] = jnp.full((8, 128), dt * react_ref[f * fields + e] + own)

        at = pl.ds(pl.multiple_of(f * 8, 8), 8)
        low_y, high_y = layers[2, at, :], layers[3, at, :]
        low_z = layers[4, at, :] * (rate + minus[2])
        high_z = layers[5, at, :] * (rate + plus[2])
        for ii in range(4):
            ends[0, f, ii] = pltpu.roll(low_y, 128 - 32 * ii, 1) if ii else low_y
            ends[1, f, ii] = pltpu.roll(high_y, 96 - 32 * ii, 1) if ii != 3 else high_y
        for ii in range(4):
            for jj in range(8):
                n = ii * 8 + jj
                low = pltpu.roll(low_z, 128 - n, 1) if n else low_z
                high = pltpu.roll(high_z, 31 - n, 1) if n != 31 else high_z
                ghost[f, ii, jj] = jnp.where(at_low_z, low, jnp.where(at_high_z, high, 0.0))
                plane = rows[plane_rows(fields, f, ii, jj), :]
                u[0, f, ii + 1, jj + 1] = plane
                if ii == 0:
                    u[0, f, 5, jj + 1] = halo_high_x(plane, f, jj)
                if ii == 3:
                    u[0, f, 0, jj + 1] = halo_low_x(plane, f, jj)
                if jj == 0:
                    u[0, f, ii + 1, 9] = halo_high_y(plane, f, ii)
                if jj == 7:
                    u[0, f, ii + 1, 0] = halo_low_y(plane, f, ii)
        return carry

    lax.fori_loop(0, fields, prepare, 0)

    def substep(index, carry):
        now = index % 2
        later = 1 - now

        def planes(jj, inner):
            mid = [[u[now, f, ii + 1, jj + 1] for ii in range(4)] for f in range(fields)]
            for f in range(fields):
                before = [u[now, f, 0, jj + 1]] + mid[f][:-1]
                after = mid[f][1:] + [u[now, f, 5, jj + 1]]
                total = []
                for ii in range(4):
                    c = mid[f][ii]
                    v = ghost[f, ii, jj] + coef[f, 0] * before[ii]
                    v = v + coef[f, 1] * after[ii]
                    v = v + coef[f, 2] * u[now, f, ii + 1, jj]
                    v = v + coef[f, 3] * u[now, f, ii + 1, jj + 2]
                    v = v + coef[f, 4] * pltpu.roll(c, 1, 1)
                    v = v + coef[f, 5] * pltpu.roll(c, 127, 1)
                    total.append(v)
                for e in range(fields):
                    weight = coef[f, 6 + e]
                    for ii in range(4):
                        total[ii] = total[ii] + weight * mid[e][ii]
                for ii in range(4):
                    u[later, f, ii + 1, jj + 1] = total[ii]
                u[later, f, 5, jj + 1] = halo_high_x(total[0], f, jj)
                u[later, f, 0, jj + 1] = halo_low_x(total[3], f, jj)
            return inner

        lax.fori_loop(0, 8, planes, 0)

        def halos(f, inner):
            for ii in range(4):
                u[later, f, ii + 1, 9] = halo_high_y(u[later, f, ii + 1, 1], f, ii)
                u[later, f, ii + 1, 0] = halo_low_y(u[later, f, ii + 1, 8], f, ii)
            return inner

        lax.fori_loop(0, fields, halos, 0, unroll=5)
        return carry

    lax.fori_loop(0, substeps, substep, 0)
    last = substeps % 2
    height = fields * 32

    def finish(f, carry):
        for ii in range(4):
            for jj in range(8):
                rows[plane_rows(fields, f, ii, jj), :] = u[last, f, ii + 1, jj + 1]
        return carry

    lax.fori_loop(0, fields, finish, 0)
    for half in range(2):
        tiles = []
        for g in range(4):
            at = (half * 4 + g) * height
            tiles.append(rows[at : at + height, :].astype(jnp.bfloat16))
        moved = jnp.dot(
            jnp.concatenate(tiles, axis=1), matrix[...], preferred_element_type=jnp.float32
        ).astype(jnp.bfloat16)
        for m in range(4):
            at = 128 * (half + 2 * m)
            o_ref[0, :, :, at : at + 128] = moved[:, 128 * m : 128 * m + 128].reshape(
                fields, 32, 128
            )


def advance(blocks, faces, meta, count, scalars, out_blocks):
    per_dev, fields, cells, plane = blocks.shape
    block_shape = (1, fields, cells, plane)
    picked = lambda g, meta, *_: (meta[g], 0, 0, 0)
    return pl.pallas_call(
        advance_kernel,
        grid_spec=pltpu.PrefetchScalarGridSpec(
            num_scalar_prefetch=4,
            grid=(count,),
            in_specs=[
                pl.BlockSpec(block_shape, picked),
                pl.BlockSpec(faces.shape, lambda g, *_: (0, 0, 0)),
            ],
            out_specs=pl.BlockSpec(
                block_shape, picked if out_blocks > 1 else lambda g, *_: (0, 0, 0, 0)
            ),
            scratch_shapes=[
                pltpu.VMEM((2, fields, 6, 10, 8, 128), jnp.float32),
                pltpu.VMEM((fields, 4, 8, 8, 128), jnp.float32),
                pltpu.VMEM((6, fields * 8, 128), jnp.float32),
                pltpu.VMEM((2, fields, 4, 8, 128), jnp.float32),
                pltpu.VMEM((fields, 6 + fields, 8, 128), jnp.float32),
                pltpu.VMEM((fields * 256, 128), jnp.float32),
                pltpu.VMEM((512, 512), jnp.bfloat16),
            ],
        ),
        out_shape=jax.ShapeDtypeStruct((out_blocks, fields, cells, plane), jnp.bfloat16),
        compiler_params=pltpu.CompilerParams(vmem_limit_bytes=VMEM_LIMIT),
        cost_estimate=pl.CostEstimate(
            flops=count * 40_000_000_000, bytes_accessed=count * 1_400_000, transcendentals=0
        ),
    )(meta, *scalars, blocks, faces)


def local(
    block_state,
    block_level,
    block_velocity,
    diffusivity,
    reaction_matrix,
    ghost_source,
    swap_bit,
    swap_slot,
):
    blocks = block_state[0]
    per_dev = blocks.shape[0]
    requests = per_dev * 6
    peers = lax.axis_size(("gy", "gz"))
    my_index = lax.axis_index(("gy", "gz"))
    base = my_index * per_dev
    wanted = ghost_source[0].reshape(peers, requests)
    order = jnp.arange(requests, dtype=jnp.int32)[None, :]
    code = order * 64 + wanted % per_dev * 6 + (order % 6 ^ 1)
    match = wanted // per_dev == my_index
    first = jnp.min(jnp.where(match, code, requests * 64), axis=1)
    final = jnp.max(jnp.where(match, code, 0), axis=1)
    sel = jnp.stack([first, final], axis=1).reshape(2 * peers) % 64

    outgoing = pack_faces(blocks, sel)
    arrived = lax.all_to_all(outgoing, ("gy", "gz"), split_axis=0, concat_axis=0, tiled=True)

    slot_here = swap_slot[0, 0, 0]
    bit_here = swap_bit[0, 0, 0]
    levels = block_level[0]
    mine = lax.dynamic_index_in_dim(wanted, my_index, 0, keepdims=False)
    source_dev = mine // per_dev
    earlier = jnp.arange(requests)[None, :] < jnp.arange(requests)[:, None]
    second = jnp.any((source_dev[:, None] == source_dev[None, :]) & earlier, axis=1)
    lookup = source_dev * 2 + second.astype(jnp.int32)
    own_levels = lax.dynamic_slice_in_dim(levels, base, per_dev, 0)
    numbers = jnp.arange(levels.shape[0], dtype=jnp.int32)
    donor_levels = jnp.sum(
        jnp.where(mine[:, None] == numbers[None, :], levels[None, :], 0), axis=1
    )
    differs = (donor_levels != jnp.repeat(own_levels, 6)).astype(jnp.int32)
    others = jnp.arange(per_dev, dtype=jnp.int32)
    others = (others + (others >= slot_here).astype(jnp.int32)) % per_dev
    tail = jnp.concatenate([own_levels, lookup, differs])
    meta_first = jnp.concatenate([jnp.full((per_dev,), slot_here), tail])
    meta_rest = jnp.concatenate([others, tail])
    scalars = (
        block_velocity[0].astype(jnp.float32).reshape(-1),
        diffusivity,
        reaction_matrix.reshape(-1),
    )
    departing = advance(blocks, arrived, meta_first, 1, scalars, 1)
    bit_count = lax.axis_size("gx").bit_length() - 1
    partners = [swapped(departing, "gx", bit_no) for bit_no in range(bit_count)]
    rest = advance(blocks, arrived, meta_rest, per_dev - 1, scalars, per_dev)
    coming = departing
    for bit_no in range(bit_count):
        coming = jnp.where(bit_here == bit_no, partners[bit_no], coming)
    result = lax.dynamic_update_index_in_dim(rest, coming[0], slot_here, 0)
    return result[None]


def solution(mesh):
    in_specs = (
        P("gx", ("gy", "gz"), None, None, None),
        P("gx", None),
        P("gx", ("gy", "gz"), None),
        P(),
        P(),
        P("gx", None, None),
        P("gx", "gy", "gz"),
        P("gx", "gy", "gz"),
    )
    out_specs = P("gx", ("gy", "gz"), None, None, None)
    return jax.shard_map(local, mesh=mesh, in_specs=in_specs, out_specs=out_specs, check_vma=False)
```

```python
import functools

import jax
import jax.numpy as jnp
from jax import lax
from jax.experimental import pallas as pl
from jax.experimental.pallas import tpu as pltpu
from jax.sharding import PartitionSpec as P

dt_base = 0.05
VMEM_LIMIT = 56 * 1024 * 1024


def swapped(x, axis, bit):
    return lax.ppermute(x, axis, [(i, i ^ 1 << bit) for i in range(lax.axis_size(axis))])


def lane_iota():
    return lax.broadcasted_iota(jnp.int32, (8, 128), 1)


def row_iota():
    return lax.broadcasted_iota(jnp.int32, (8, 128), 0)


def regroup_matrix():
    r = lax.broadcasted_iota(jnp.int32, (512, 512), 0)
    c = lax.broadcasted_iota(jnp.int32, (512, 512), 1)
    target = (r // 32) % 4 * 128 + r // 128 * 32 + r % 32
    return jnp.where(c == target, 1.0, 0.0).astype(jnp.bfloat16)


def regroup_in(x_ref, matrix, rows):
    fields = x_ref.shape[1]
    height = fields * 32
    for half in range(2):
        tiles = [
            x_ref[0, :, :, 128 * (half + 2 * m) : 128 * (half + 2 * m) + 128].reshape(height, 128)
            for m in range(4)
        ]
        moved = jnp.dot(
            jnp.concatenate(tiles, axis=1), matrix[...], preferred_element_type=jnp.float32
        )
        for g in range(4):
            at = (half * 4 + g) * height
            rows[at : at + height, :] = moved[:, 128 * g : 128 * g + 128]


def plane_rows(fields, f, ii, jj):
    return pl.ds(jj * fields * 32 + f * 32 + ii, 8, stride=4)


def pack_kernel(sel_ref, x_ref, out_ref, faces, rows, matrix):
    step = pl.program_id(0)
    fields = x_ref.shape[1]
    lane = lane_iota()
    k = lane % 32

    @pl.when(step == 0)
    def _():
        matrix[...] = regroup_matrix()

    regroup_in(x_ref, matrix, rows)

    def pair(fp, carry):
        got = [[], [], [], [], [], []]
        for half in range(2):
            f = fp * 2 + half
            got[0].append(rows[pl.ds(f * 32, 8, stride=fields * 32), :])
            got[1].append(rows[pl.ds(f * 32 + 31, 8, stride=fields * 32), :])
            low_y = high_y = low_z = high_z = jnp.zeros((8, 128), jnp.float32)
            for ii in range(4):
                for jj in range(8):
                    plane = rows[plane_rows(fields, f, ii, jj), :]
                    n = ii * 8 + jj
                    here = k == n
                    low_z = jnp.where(here, pltpu.roll(plane, n, 1) if n else plane, low_z)
                    high_z = jnp.where(
                        here, pltpu.roll(plane, n + 97, 1) if n != 31 else plane, high_z
                    )
                    here = lane // 32 == ii
                    if jj == 0:
                        low_y = jnp.where(here, pltpu.roll(plane, 32 * ii, 1) if ii else plane, low_y)
                    if jj == 7:
                        moved = pltpu.roll(plane, 32 * ii + 32, 1) if ii != 3 else plane
                        high_y = jnp.where(here, moved, high_y)
            got[2].append(low_y)
            got[3].append(high_y)
            got[4].append(low_z)
            got[5].append(high_z)
        at = fp * 16
        for face in range(6):
            both = jnp.concatenate(got[face], axis=0).astype(jnp.bfloat16)
            faces[step * 6 + face, pl.ds(at, 16), :] = both
        return carry

    for fp in range(fields // 2):
        pair(fp, 0)

    @pl.when(step == pl.num_programs(0) - 1)
    def _():
        def place(n, carry):
            out_ref[n] = faces[sel_ref[n]]
            return carry

        lax.fori_loop(0, out_ref.shape[0], place, 0, unroll=4)


def pack_faces(blocks, sel):
    per_dev, fields, cells, plane = blocks.shape
    return pl.pallas_call(
        pack_kernel,
        grid_spec=pltpu.PrefetchScalarGridSpec(
            num_scalar_prefetch=1,
            grid=(per_dev,),
            in_specs=[pl.BlockSpec((1, fields, cells, plane), lambda g, *_: (g, 0, 0, 0))],
            out_specs=pl.BlockSpec((sel.shape[0], fields * 8, 128), lambda g, *_: (0, 0, 0)),
            scratch_shapes=[
                pltpu.VMEM((per_dev * 6, fields * 8, 128), jnp.bfloat16),
                pltpu.VMEM((fields * 256, 128), jnp.float32),
                pltpu.VMEM((512, 512), jnp.bfloat16),
            ],
        ),
        out_shape=jax.ShapeDtypeStruct((sel.shape[0], fields * 8, 128), jnp.bfloat16),
        compiler_params=pltpu.CompilerParams(vmem_limit_bytes=VMEM_LIMIT),
    )(sel, blocks)


def pair_sum(x, distance, axis, bit_clear):
    size = x.shape[axis]
    other = jnp.where(
        bit_clear, pltpu.roll(x, size - distance, axis), pltpu.roll(x, distance, axis)
    )
    return x + other


def advance_kernel(
    meta_ref, speed_ref, rate_ref,
    react_ref, centre_ref, x_ref, faces_ref, o_ref,
    u, ghost, layers, ends, coef, mixer, rows, matrix,
):
    fields = x_ref.shape[1]
    step = pl.program_id(0)
    count = pl.num_programs(0)
    per_dev = speed_ref.shape[0] // 3
    requests = per_dev * 6
    block = meta_ref[step]
    own_level = meta_ref[per_dev + block]
    substeps = jnp.left_shift(jnp.int32(1), own_level)
    scale = substeps.astype(jnp.float32)
    dt = jnp.where(own_level == 0, dt_base, jnp.where(own_level == 1, dt_base / 2, dt_base / 4))
    lane, row = lane_iota(), row_iota()
    k = lane % 32
    at_low_z, at_high_z = k == 0, k == 31

    @pl.when(step == 0)
    def _():
        matrix[...] = regroup_matrix()

    regroup_in(x_ref, matrix, rows)

    tall_lane = lax.broadcasted_iota(jnp.int32, (fields * 8, 128), 1)
    tall_row = lax.broadcasted_iota(jnp.int32, (fields * 8, 128), 0)
    for face in range(6):
        request = block * 6 + face
        layers[face] = faces_ref[meta_ref[2 * per_dev + request]].astype(jnp.float32)

        @pl.when(meta_ref[2 * per_dev + requests + request] > 0)
        def _():
            v = pair_sum(layers[face], 1, 1, tall_lane % 2 == 0)
            if face < 2:
                v = pair_sum(v, 1, 0, tall_row % 2 == 0)
            elif face < 4:
                v = pair_sum(v, 32, 1, tall_lane // 32 % 2 == 0)
            else:
                v = pair_sum(v, 8, 1, tall_lane // 8 % 2 == 0)
            layers[face] = v * 0.25

    speeds = [speed_ref[block * 3 + d] for d in range(3)]
    minus = [jnp.maximum(v, 0.0) * scale * dt for v in speeds]
    plus = [-jnp.minimum(v, 0.0) * scale * dt for v in speeds]
    outflow = minus[0] + plus[0] + minus[1] + plus[1] + minus[2] + plus[2]

    def halo_low_x(plane, f, jj):
        edge = layers[0, pl.ds(f * 8 + jj, 1), :]
        return jnp.where(row == 0, edge, pltpu.roll(plane, 1, 0))

    def halo_high_x(plane, f, jj):
        edge = layers[1, pl.ds(f * 8 + jj, 1), :]
        return jnp.where(row == 7, edge, pltpu.roll(plane, 7, 0))

    def halo_low_y(plane, f, ii):
        return jnp.where(lane < 32, ends[0, f, ii], pltpu.roll(plane, 32, 1))

    def halo_high_y(plane, f, ii):
        return jnp.where(lane >= 96, ends[1, f, ii], pltpu.roll(plane, 96, 1))

    def prepare(f, carry):
        rate = rate_ref[f] * (scale * scale) * dt
        coef[f, 0] = jnp.full((8, 128), rate + minus[0])
        coef[f, 1] = jnp.full((8, 128), rate + plus[0])
        coef[f, 2] = jnp.full((8, 128), rate + minus[1])
        coef[f, 3] = jnp.full((8, 128), rate + plus[1])
        coef[f, 4] = jnp.where(at_low_z, 0.0, rate + minus[2])
        coef[f, 5] = jnp.where(at_high_z, 0.0, rate + plus[2])

        at = pl.ds(pl.multiple_of(f * 8, 8), 8)
        low_y, high_y = layers[2, at, :], layers[3, at, :]
        low_z = layers[4, at, :] * (rate + minus[2])
        high_z = layers[5, at, :] * (rate + plus[2])
        for ii in range(4):
            ends[0, f, ii] = pltpu.roll(low_y, 128 - 32 * ii, 1) if ii else low_y
            ends[1, f, ii] = pltpu.roll(high_y, 96 - 32 * ii, 1) if ii != 3 else high_y
        for ii in range(4):
            for jj in range(8):
                n = ii * 8 + jj
                low = pltpu.roll(low_z, 128 - n, 1) if n else low_z
                high = pltpu.roll(high_z, 31 - n, 1) if n != 31 else high_z
                ghost[f, ii, jj] = jnp.where(at_low_z, low, jnp.where(at_high_z, high, 0.0))
                plane = rows[plane_rows(fields, f, ii, jj), :]
                u[0, f, ii + 1, jj + 1] = plane
                if ii == 0:
                    u[0, f, 5, jj + 1] = halo_high_x(plane, f, jj)
                if ii == 3:
                    u[0, f, 0, jj + 1] = halo_low_x(plane, f, jj)
                if jj == 0:
                    u[0, f, ii + 1, 9] = halo_high_y(plane, f, ii)
                if jj == 7:
                    u[0, f, ii + 1, 0] = halo_low_y(plane, f, ii)
        return carry

    lax.fori_loop(0, fields, prepare, 0, unroll=2)

    height8 = fields * 8
    wide_row = lax.broadcasted_iota(jnp.int32, (height8, 3 * height8), 0)
    wide_lane = lax.broadcasted_iota(jnp.int32, (height8, 3 * height8), 1)
    own = jnp.where(wide_lane % height8 == wide_row, 1.0 - outflow, 0.0)
    mix = react_ref[...] * dt + own - centre_ref[...] * (6.0 * scale * scale * dt)
    mix_high = mix.astype(jnp.bfloat16)
    mix_low = (mix - mix_high.astype(jnp.float32)).astype(jnp.bfloat16)
    mixer[...] = jnp.where(wide_lane < 2 * height8, mix_high, mix_low)

    def substep(index, carry):
        now = index % 2
        later = 1 - now

        def planes(jj, inner):
            columns = []
            for ii in range(4):
                value = jnp.concatenate(
                    [u[now, f, ii + 1, jj + 1] for f in range(fields)], axis=0
                )
                high = value.astype(jnp.bfloat16)
                low = (value - high.astype(jnp.float32)).astype(jnp.bfloat16)
                columns.append(jnp.concatenate([high, low, high], axis=0))
            mixed = jnp.dot(
                mixer[...], jnp.concatenate(columns, axis=1), preferred_element_type=jnp.float32
            )
            for f in range(fields):
                mid = [u[now, f, ii + 1, jj + 1] for ii in range(4)]
                before = [u[now, f, 0, jj + 1]] + mid[:-1]
                after = mid[1:] + [u[now, f, 5, jj + 1]]
                total = []
                for ii in range(4):
                    c = mid[ii]
                    v = mixed[8 * f : 8 * f + 8, 128 * ii : 128 * ii + 128] + ghost[f, ii, jj]
                    v = v + coef[f, 0] * before[ii]
                    v = v + coef[f, 1] * after[ii]
                    v = v + coef[f, 2] * u[now, f, ii + 1, jj]
                    v = v + coef[f, 3] * u[now, f, ii + 1, jj + 2]
                    v = v + coef[f, 4] * pltpu.roll(c, 1, 1)
                    v = v + coef[f, 5] * pltpu.roll(c, 127, 1)
                    total.append(v)
                for ii in range(4):
                    u[later, f, ii + 1, jj + 1] = total[ii]
                u[later, f, 5, jj + 1] = halo_high_x(total[0], f, jj)
                u[later, f, 0, jj + 1] = halo_low_x(total[3], f, jj)
            return inner

        lax.fori_loop(0, 8, planes, 0, unroll=2)

        def halos(f, inner):
            for ii in range(4):
                u[later, f, ii + 1, 9] = halo_high_y(u[later, f, ii + 1, 1], f, ii)
                u[later, f, ii + 1, 0] = halo_low_y(u[later, f, ii + 1, 8], f, ii)
            return inner

        lax.fori_loop(0, fields, halos, 0, unroll=5)
        return carry

    lax.fori_loop(0, substeps, substep, 0)
    last = substeps % 2
    height = fields * 32

    def finish(f, carry):
        for ii in range(4):
            for jj in range(8):
                rows[plane_rows(fields, f, ii, jj), :] = u[last, f, ii + 1, jj + 1]
        return carry

    lax.fori_loop(0, fields, finish, 0)
    for half in range(2):
        tiles = []
        for g in range(4):
            at = (half * 4 + g) * height
            tiles.append(rows[at : at + height, :].astype(jnp.bfloat16))
        moved = jnp.dot(
            jnp.concatenate(tiles, axis=1), matrix[...], preferred_element_type=jnp.float32
        ).astype(jnp.bfloat16)
        for m in range(4):
            at = 128 * (half + 2 * m)
            o_ref[0, :, :, at : at + 128] = moved[:, 128 * m : 128 * m + 128].reshape(
                fields, 32, 128
            )


def advance(blocks, faces, meta, count, scalars, out_blocks):
    per_dev, fields, cells, plane = blocks.shape
    block_shape = (1, fields, cells, plane)
    picked = lambda g, meta, *_: (meta[g], 0, 0, 0)
    return pl.pallas_call(
        advance_kernel,
        grid_spec=pltpu.PrefetchScalarGridSpec(
            num_scalar_prefetch=3,
            grid=(count,),
            in_specs=[
                pl.BlockSpec((fields * 8, fields * 24), lambda g, *_: (0, 0)),
                pl.BlockSpec((fields * 8, fields * 24), lambda g, *_: (0, 0)),
                pl.BlockSpec(block_shape, picked),
                pl.BlockSpec(faces.shape, lambda g, *_: (0, 0, 0)),
            ],
            out_specs=pl.BlockSpec(
                block_shape, picked if out_blocks > 1 else lambda g, *_: (0, 0, 0, 0)
            ),
            scratch_shapes=[
                pltpu.VMEM((2, fields, 6, 10, 8, 128), jnp.float32),
                pltpu.VMEM((fields, 4, 8, 8, 128), jnp.float32),
                pltpu.VMEM((6, fields * 8, 128), jnp.float32),
                pltpu.VMEM((2, fields, 4, 8, 128), jnp.float32),
                pltpu.VMEM((fields, 6, 8, 128), jnp.float32),
                pltpu.VMEM((fields * 8, fields * 24), jnp.bfloat16),
                pltpu.VMEM((fields * 256, 128), jnp.float32),
                pltpu.VMEM((512, 512), jnp.bfloat16),
            ],
        ),
        out_shape=jax.ShapeDtypeStruct((out_blocks, fields, cells, plane), jnp.bfloat16),
        compiler_params=pltpu.CompilerParams(vmem_limit_bytes=VMEM_LIMIT),
        cost_estimate=pl.CostEstimate(
            flops=count * 40_000_000_000, bytes_accessed=count * 1_400_000, transcendentals=0
        ),
    )(meta, *scalars, blocks, faces)


def local(
    block_state,
    block_level,
    block_velocity,
    diffusivity,
    reaction_matrix,
    ghost_source,
    swap_bit,
    swap_slot,
):
    blocks = block_state[0]
    per_dev = blocks.shape[0]
    requests = per_dev * 6
    peers = lax.axis_size(("gy", "gz"))
    my_index = lax.axis_index(("gy", "gz"))
    base = my_index * per_dev
    wanted = ghost_source[0].reshape(peers, requests)
    order = jnp.arange(requests, dtype=jnp.int32)[None, :]
    code = order * 64 + wanted % per_dev * 6 + (order % 6 ^ 1)
    match = wanted // per_dev == my_index
    first = jnp.min(jnp.where(match, code, requests * 64), axis=1)
    final = jnp.max(jnp.where(match, code, 0), axis=1)
    sel = jnp.stack([first, final], axis=1).reshape(2 * peers) % 64

    outgoing = pack_faces(blocks, sel)
    arrived = lax.all_to_all(outgoing, ("gy", "gz"), split_axis=0, concat_axis=0, tiled=True)

    slot_here = swap_slot[0, 0, 0]
    bit_here = swap_bit[0, 0, 0]
    levels = block_level[0]
    mine = lax.dynamic_index_in_dim(wanted, my_index, 0, keepdims=False)
    source_dev = mine // per_dev
    earlier = jnp.arange(requests)[None, :] < jnp.arange(requests)[:, None]
    second = jnp.any((source_dev[:, None] == source_dev[None, :]) & earlier, axis=1)
    lookup = source_dev * 2 + second.astype(jnp.int32)
    own_levels = lax.dynamic_slice_in_dim(levels, base, per_dev, 0)
    numbers = jnp.arange(levels.shape[0], dtype=jnp.int32)
    donor_levels = jnp.sum(
        jnp.where(mine[:, None] == numbers[None, :], levels[None, :], 0), axis=1
    )
    differs = (donor_levels != jnp.repeat(own_levels, 6)).astype(jnp.int32)
    others = jnp.arange(per_dev, dtype=jnp.int32)
    others = (others + (others >= slot_here).astype(jnp.int32)) % per_dev
    tail = jnp.concatenate([own_levels, lookup, differs])
    meta_first = jnp.concatenate([jnp.full((per_dev,), slot_here), tail])
    meta_rest = jnp.concatenate([others, tail])
    scalars = (
        block_velocity[0].astype(jnp.float32).reshape(-1),
        diffusivity,
        jnp.tile(jnp.kron(reaction_matrix, jnp.eye(8)), (1, 3)),
        jnp.tile(jnp.diag(jnp.repeat(diffusivity, 8)), (1, 3)),
    )
    departing = advance(blocks, arrived, meta_first, 1, scalars, 1)
    bit_count = lax.axis_size("gx").bit_length() - 1
    partners = [swapped(departing, "gx", bit_no) for bit_no in range(bit_count)]
    rest = advance(blocks, arrived, meta_rest, per_dev - 1, scalars, per_dev)
    coming = departing
    for bit_no in range(bit_count):
        coming = jnp.where(bit_here == bit_no, partners[bit_no], coming)
    result = lax.dynamic_update_index_in_dim(rest, coming[0], slot_here, 0)
    return result[None]


def solution(mesh):
    in_specs = (
        P("gx", ("gy", "gz"), None, None, None),
        P("gx", None),
        P("gx", ("gy", "gz"), None),
        P(),
        P(),
        P("gx", None, None),
        P("gx", "gy", "gz"),
        P("gx", "gy", "gz"),
    )
    out_specs = P("gx", ("gy", "gz"), None, None, None)
    return jax.shard_map(local, mesh=mesh, in_specs=in_specs, out_specs=out_specs, check_vma=False)
```

```python
import functools

import jax
import jax.numpy as jnp
from jax import lax
from jax.experimental import pallas as pl
from jax.experimental.pallas import tpu as pltpu
from jax.sharding import PartitionSpec as P

dt_base = 0.05
VMEM_LIMIT = 56 * 1024 * 1024


def swapped(x, axis, bit):
    return lax.ppermute(x, axis, [(i, i ^ 1 << bit) for i in range(lax.axis_size(axis))])


def lane_iota():
    return lax.broadcasted_iota(jnp.int32, (8, 128), 1)


def row_iota():
    return lax.broadcasted_iota(jnp.int32, (8, 128), 0)


def exchange_groups(tiles):
    group = lax.broadcasted_iota(jnp.int32, tiles[0].shape, 1) // 32
    odd, upper = group % 2 == 1, group >= 2
    stage = [None] * 4
    for m in (0, 2):
        stage[m] = jnp.where(odd, pltpu.roll(tiles[m + 1], 32, 1), tiles[m])
        stage[m + 1] = jnp.where(odd, tiles[m + 1], pltpu.roll(tiles[m], 96, 1))
    done = [None] * 4
    for m in (0, 1):
        done[m] = jnp.where(upper, pltpu.roll(stage[m + 2], 64, 1), stage[m])
        done[m + 2] = jnp.where(upper, stage[m + 2], pltpu.roll(stage[m], 64, 1))
    return done


def regroup_in(x_ref, f, rows):
    for half in range(2):
        tiles = []
        for m in range(4):
            at = 128 * (half + 2 * m)
            tiles.append(x_ref[0, f, :, at : at + 128].astype(jnp.float32))
        for g, tile in enumerate(exchange_groups(tiles)):
            rows[pl.ds(f * 256 + (half * 4 + g) * 32, 32), :] = tile


def plane_rows(f, ii, jj):
    return pl.ds(f * 256 + jj * 32 + ii, 8, stride=4)


def pack_kernel(sel_ref, x_ref, out_ref, faces, rows):
    step = pl.program_id(0)
    fields = x_ref.shape[1]
    lane = lane_iota()
    k = lane % 32

    def pair(fp, carry):
        got = [[], [], [], [], [], []]
        for half in range(2):
            f = fp * 2 + half
            regroup_in(x_ref, f, rows)
            got[0].append(rows[pl.ds(f * 256, 8, stride=32), :])
            got[1].append(rows[pl.ds(f * 256 + 31, 8, stride=32), :])
            low_y = high_y = low_z = high_z = jnp.zeros((8, 128), jnp.float32)
            for ii in range(4):
                for jj in range(8):
                    plane = rows[plane_rows(f, ii, jj), :]
                    n = ii * 8 + jj
                    here = k == n
                    low_z = jnp.where(here, pltpu.roll(plane, n, 1) if n else plane, low_z)
                    high_z = jnp.where(
                        here, pltpu.roll(plane, n + 97, 1) if n != 31 else plane, high_z
                    )
                    here = lane // 32 == ii
                    if jj == 0:
                        low_y = jnp.where(here, pltpu.roll(plane, 32 * ii, 1) if ii else plane, low_y)
                    if jj == 7:
                        moved = pltpu.roll(plane, 32 * ii + 32, 1) if ii != 3 else plane
                        high_y = jnp.where(here, moved, high_y)
            got[2].append(low_y)
            got[3].append(high_y)
            got[4].append(low_z)
            got[5].append(high_z)
        at = fp * 16
        for face in range(6):
            both = jnp.concatenate(got[face], axis=0).astype(jnp.bfloat16)
            faces[step * 6 + face, pl.ds(at, 16), :] = both
        return carry

    for fp in range(fields // 2):
        pair(fp, 0)

    @pl.when(step == pl.num_programs(0) - 1)
    def _():
        def place(n, carry):
            out_ref[n] = faces[sel_ref[n]]
            return carry

        lax.fori_loop(0, out_ref.shape[0], place, 0, unroll=4)


def pack_faces(blocks, sel):
    per_dev, fields, cells, plane = blocks.shape
    return pl.pallas_call(
        pack_kernel,
        grid_spec=pltpu.PrefetchScalarGridSpec(
            num_scalar_prefetch=1,
            grid=(per_dev,),
            in_specs=[pl.BlockSpec((1, fields, cells, plane), lambda g, *_: (g, 0, 0, 0))],
            out_specs=pl.BlockSpec((sel.shape[0], fields * 8, 128), lambda g, *_: (0, 0, 0)),
            scratch_shapes=[
                pltpu.VMEM((per_dev * 6, fields * 8, 128), jnp.bfloat16),
                pltpu.VMEM((fields * 256, 128), jnp.float32),
            ],
        ),
        out_shape=jax.ShapeDtypeStruct((sel.shape[0], fields * 8, 128), jnp.bfloat16),
        compiler_params=pltpu.CompilerParams(vmem_limit_bytes=VMEM_LIMIT),
    )(sel, blocks)


def pair_sum(x, distance, axis, bit_clear):
    size = x.shape[axis]
    other = jnp.where(
        bit_clear, pltpu.roll(x, size - distance, axis), pltpu.roll(x, distance, axis)
    )
    return x + other


def advance_kernel(
    meta_ref, speed_ref, rate_ref, react_ref,
    x_ref, faces_ref, o_ref,
    u, ghost, layers, ends, coef, rows,
):
    fields = x_ref.shape[1]
    step = pl.program_id(0)
    per_dev = speed_ref.shape[0] // 3
    requests = per_dev * 6
    block = meta_ref[step]
    own_level = meta_ref[per_dev + block]
    substeps = jnp.left_shift(jnp.int32(1), own_level)
    scale = substeps.astype(jnp.float32)
    dt = jnp.where(own_level == 0, dt_base, jnp.where(own_level == 1, dt_base / 2, dt_base / 4))
    lane, row = lane_iota(), row_iota()
    k = lane % 32
    at_low_z, at_high_z = k == 0, k == 31

    tall_lane = lax.broadcasted_iota(jnp.int32, (fields * 8, 128), 1)
    tall_row = lax.broadcasted_iota(jnp.int32, (fields * 8, 128), 0)
    for face in range(6):
        request = block * 6 + face
        layers[face] = faces_ref[meta_ref[2 * per_dev + request]].astype(jnp.float32)

        @pl.when(meta_ref[2 * per_dev + requests + request] > 0)
        def _():
            v = pair_sum(layers[face], 1, 1, tall_lane % 2 == 0)
            if face < 2:
                v = pair_sum(v, 1, 0, tall_row % 2 == 0)
            elif face < 4:
                v = pair_sum(v, 32, 1, tall_lane // 32 % 2 == 0)
            else:
                v = pair_sum(v, 8, 1, tall_lane // 8 % 2 == 0)
            layers[face] = v * 0.25

    speeds = [speed_ref[block * 3 + d] for d in range(3)]
    minus = [jnp.maximum(v, 0.0) * scale * dt for v in speeds]
    plus = [-jnp.minimum(v, 0.0) * scale * dt for v in speeds]
    outflow = minus[0] + plus[0] + minus[1] + plus[1] + minus[2] + plus[2]

    def halo_low_x(plane, f, jj):
        edge = layers[0, pl.ds(f * 8 + jj, 1), :]
        return jnp.where(row == 0, edge, pltpu.roll(plane, 1, 0))

    def halo_high_x(plane, f, jj):
        edge = layers[1, pl.ds(f * 8 + jj, 1), :]
        return jnp.where(row == 7, edge, pltpu.roll(plane, 7, 0))

    def halo_low_y(plane, f, ii):
        return jnp.where(lane < 32, ends[0, f, ii], pltpu.roll(plane, 32, 1))

    def halo_high_y(plane, f, ii):
        return jnp.where(lane >= 96, ends[1, f, ii], pltpu.roll(plane, 96, 1))

    def prepare(f, carry):
        regroup_in(x_ref, f, rows)
        rate = rate_ref[f] * (scale * scale) * dt
        coef[f, 0] = jnp.full((8, 128), rate + minus[0])
        coef[f, 1] = jnp.full((8, 128), rate + plus[0])
        coef[f, 2] = jnp.full((8, 128), rate + minus[1])
        coef[f, 3] = jnp.full((8, 128), rate + plus[1])
        coef[f, 4] = jnp.where(at_low_z, 0.0, rate + minus[2])
        coef[f, 5] = jnp.where(at_high_z, 0.0, rate + plus[2])
        for e in range(fields):
            own = jnp.where(f == e, 1.0 - 6.0 * rate - outflow, 0.0)
            coef[f, 6 + e] = jnp.full((8, 128), dt * react_ref[f * fields + e] + own)

        at = pl.ds(pl.multiple_of(f * 8, 8), 8)
        low_y, high_y = layers[2, at, :], layers[3, at, :]
        low_z = layers[4, at, :] * (rate + minus[2])
        high_z = layers[5, at, :] * (rate + plus[2])
        for ii in range(4):
            ends[0, f, ii] = pltpu.roll(low_y, 128 - 32 * ii, 1) if ii else low_y
            ends[1, f, ii] = pltpu.roll(high_y, 96 - 32 * ii, 1) if ii != 3 else high_y
        for ii in range(4):
            for jj in range(8):
                n = ii * 8 + jj
                low = pltpu.roll(low_z, 128 - n, 1) if n else low_z
                high = pltpu.roll(high_z, 31 - n, 1) if n != 31 else high_z
                ghost[f, ii, jj] = jnp.where(at_low_z, low, jnp.where(at_high_z, high, 0.0))
                plane = rows[plane_rows(f, ii, jj), :]
                u[0, f, ii + 1, jj + 1] = plane
                if ii == 0:
                    u[0, f, 5, jj + 1] = halo_high_x(plane, f, jj)
                if ii == 3:
                    u[0, f, 0, jj + 1] = halo_low_x(plane, f, jj)
                if jj == 0:
                    u[0, f, ii + 1, 9] = halo_high_y(plane, f, ii)
                if jj == 7:
                    u[0, f, ii + 1, 0] = halo_low_y(plane, f, ii)
        return carry

    lax.fori_loop(0, fields, prepare, 0, unroll=2)

    def substep(index, carry):
        now = index % 2
        later = 1 - now

        def planes(jj, inner):
            mid = [[u[now, f, ii + 1, jj + 1] for ii in range(4)] for f in range(fields)]
            for f in range(fields):
                before = [u[now, f, 0, jj + 1]] + mid[f][:-1]
                after = mid[f][1:] + [u[now, f, 5, jj + 1]]
                total = []
                for ii in range(4):
                    c = mid[f][ii]
                    v = ghost[f, ii, jj] + coef[f, 0] * before[ii]
                    v = v + coef[f, 1] * after[ii]
                    v = v + coef[f, 2] * u[now, f, ii + 1, jj]
                    v = v + coef[f, 3] * u[now, f, ii + 1, jj + 2]
                    v = v + coef[f, 4] * pltpu.roll(c, 1, 1)
                    v = v + coef[f, 5] * pltpu.roll(c, 127, 1)
                    total.append(v)
                for e in range(fields):
                    weight = coef[f, 6 + e]
                    for ii in range(4):
                        total[ii] = total[ii] + weight * mid[e][ii]
                for ii in range(4):
                    u[later, f, ii + 1, jj + 1] = total[ii]
                u[later, f, 5, jj + 1] = halo_high_x(total[0], f, jj)
                u[later, f, 0, jj + 1] = halo_low_x(total[3], f, jj)
            return inner

        lax.fori_loop(0, 8, planes, 0, unroll=2)

        def halos(f, inner):
            for ii in range(4):
                u[later, f, ii + 1, 9] = halo_high_y(u[later, f, ii + 1, 1], f, ii)
                u[later, f, ii + 1, 0] = halo_low_y(u[later, f, ii + 1, 8], f, ii)
            return inner

        lax.fori_loop(0, fields, halos, 0, unroll=5)
        return carry

    lax.fori_loop(0, substeps, substep, 0)
    last = substeps % 2

    def finish(f, carry):
        for ii in range(4):
            for jj in range(8):
                rows[plane_rows(f, ii, jj), :] = u[last, f, ii + 1, jj + 1]
        for half in range(2):
            tiles = [rows[pl.ds(f * 256 + (half * 4 + g) * 32, 32), :] for g in range(4)]
            for m, tile in enumerate(exchange_groups(tiles)):
                at = 128 * (half + 2 * m)
                o_ref[0, f, :, at : at + 128] = tile.astype(jnp.bfloat16)
        return carry

    lax.fori_loop(0, fields, finish, 0, unroll=2)


def advance(blocks, faces, meta, count, scalars, out_blocks):
    per_dev, fields, cells, plane = blocks.shape
    block_shape = (1, fields, cells, plane)
    picked = lambda g, meta, *_: (meta[g], 0, 0, 0)
    return pl.pallas_call(
        advance_kernel,
        grid_spec=pltpu.PrefetchScalarGridSpec(
            num_scalar_prefetch=4,
            grid=(count,),
            in_specs=[
                pl.BlockSpec(block_shape, picked),
                pl.BlockSpec(faces.shape, lambda g, *_: (0, 0, 0)),
            ],
            out_specs=pl.BlockSpec(
                block_shape, picked if out_blocks > 1 else lambda g, *_: (0, 0, 0, 0)
            ),
            scratch_shapes=[
                pltpu.VMEM((2, fields, 6, 10, 8, 128), jnp.float32),
                pltpu.VMEM((fields, 4, 8, 8, 128), jnp.float32),
                pltpu.VMEM((6, fields * 8, 128), jnp.float32),
                pltpu.VMEM((2, fields, 4, 8, 128), jnp.float32),
                pltpu.VMEM((fields, 6 + fields, 8, 128), jnp.float32),
                pltpu.VMEM((fields * 256, 128), jnp.float32),
            ],
        ),
        out_shape=jax.ShapeDtypeStruct((out_blocks, fields, cells, plane), jnp.bfloat16),
        compiler_params=pltpu.CompilerParams(vmem_limit_bytes=VMEM_LIMIT),
        cost_estimate=pl.CostEstimate(
            flops=count * 40_000_000_000, bytes_accessed=count * 1_400_000, transcendentals=0
        ),
    )(meta, *scalars, blocks, faces)


def local(
    block_state,
    block_level,
    block_velocity,
    diffusivity,
    reaction_matrix,
    ghost_source,
    swap_bit,
    swap_slot,
):
    blocks = block_state[0]
    per_dev = blocks.shape[0]
    requests = per_dev * 6
    peers = lax.axis_size(("gy", "gz"))
    my_index = lax.axis_index(("gy", "gz"))
    base = my_index * per_dev
    wanted = ghost_source[0].reshape(peers, requests)
    order = jnp.arange(requests, dtype=jnp.int32)[None, :]
    code = order * 64 + wanted % per_dev * 6 + (order % 6 ^ 1)
    match = wanted // per_dev == my_index
    first = jnp.min(jnp.where(match, code, requests * 64), axis=1)
    final = jnp.max(jnp.where(match, code, 0), axis=1)
    sel = jnp.stack([first, final], axis=1).reshape(2 * peers) % 64

    outgoing = pack_faces(blocks, sel)
    arrived = lax.all_to_all(outgoing, ("gy", "gz"), split_axis=0, concat_axis=0, tiled=True)

    slot_here = swap_slot[0, 0, 0]
    bit_here = swap_bit[0, 0, 0]
    levels = block_level[0]
    mine = lax.dynamic_index_in_dim(wanted, my_index, 0, keepdims=False)
    source_dev = mine // per_dev
    earlier = jnp.arange(requests)[None, :] < jnp.arange(requests)[:, None]
    second = jnp.any((source_dev[:, None] == source_dev[None, :]) & earlier, axis=1)
    lookup = source_dev * 2 + second.astype(jnp.int32)
    own_levels = lax.dynamic_slice_in_dim(levels, base, per_dev, 0)
    numbers = jnp.arange(levels.shape[0], dtype=jnp.int32)
    donor_levels = jnp.sum(
        jnp.where(mine[:, None] == numbers[None, :], levels[None, :], 0), axis=1
    )
    differs = (donor_levels != jnp.repeat(own_levels, 6)).astype(jnp.int32)
    others = jnp.arange(per_dev, dtype=jnp.int32)
    others = (others + (others >= slot_here).astype(jnp.int32)) % per_dev
    tail = jnp.concatenate([own_levels, lookup, differs])
    meta_first = jnp.concatenate([jnp.full((per_dev,), slot_here), tail])
    meta_rest = jnp.concatenate([others, tail])
    scalars = (
        block_velocity[0].astype(jnp.float32).reshape(-1),
        diffusivity,
        reaction_matrix.reshape(-1),
    )
    departing = advance(blocks, arrived, meta_first, 1, scalars, 1)
    bit_count = lax.axis_size("gx").bit_length() - 1
    partners = [swapped(departing, "gx", bit_no) for bit_no in range(bit_count)]
    rest = advance(blocks, arrived, meta_rest, per_dev - 1, scalars, per_dev)
    coming = departing
    for bit_no in range(bit_count):
        coming = jnp.where(bit_here == bit_no, partners[bit_no], coming)
    result = lax.dynamic_update_index_in_dim(rest, coming[0], slot_here, 0)
    return result[None]


def solution(mesh):
    in_specs = (
        P("gx", ("gy", "gz"), None, None, None),
        P("gx", None),
        P("gx", ("gy", "gz"), None),
        P(),
        P(),
        P("gx", None, None),
        P("gx", "gy", "gz"),
        P("gx", "gy", "gz"),
    )
    out_specs = P("gx", ("gy", "gz"), None, None, None)
    return jax.shard_map(local, mesh=mesh, in_specs=in_specs, out_specs=out_specs, check_vma=False)
```

```python
import functools

import jax
import jax.numpy as jnp
import numpy as np
from jax import lax
from jax.experimental import pallas as pl
from jax.experimental.pallas import tpu as pltpu
from jax.sharding import PartitionSpec as P

dt_base = 0.05
VMEM_LIMIT = 56 * 1024 * 1024


def swapped(x, axis, bit):
    return lax.ppermute(x, axis, [(i, i ^ 1 << bit) for i in range(lax.axis_size(axis))])


def lane_iota():
    return lax.broadcasted_iota(jnp.int32, (8, 128), 1)


def row_iota():
    return lax.broadcasted_iota(jnp.int32, (8, 128), 0)


def ones_where(mask):
    return jnp.asarray(np.where(mask, 1.0, 0.0), jnp.bfloat16)


def regroup_matrix():
    r, c = np.arange(512)[:, None], np.arange(512)[None, :]
    return ones_where(c == r // 32 % 4 * 128 + r // 128 * 32 + r % 32)


def shift_matrix():
    r, c = np.arange(256)[:, None] % 128, np.arange(256)[None, :]
    lane = c % 128
    lower = (c < 128) & (r == lane - 1) & (lane % 32 != 0)
    upper = (c >= 128) & (r == lane + 1) & (lane % 32 != 31)
    return ones_where(lower | upper)


def end_matrix():
    r, c = np.arange(512)[:, None], np.arange(1024)[None, :]
    side, j = r // 128 % 2, r % 32
    return ones_where((c // 128 + c // 32 % 4 * 8 == j) & (c % 32 == side * 31))


def face_matrix_z():
    r, c = np.arange(1024)[:, None], np.arange(256)[None, :]
    return ones_where((r // 32 == c % 32) & (r % 32 == c // 128 * 31))


def face_matrix_y():
    r, c = np.arange(256)[:, None], np.arange(256)[None, :]
    return ones_where((r // 32 == c // 128 * 7) & (r % 32 == c % 32))


def coarse_matrices():
    r, c = np.arange(128)[:, None], np.arange(128)[None, :]
    pairs = (r // 2 == c // 2) * 0.5
    patches = (r // 64 == c // 64) * (r % 32 // 2 == c % 32 // 2) * 0.25
    return jnp.asarray(np.stack([r == c, pairs, patches]).astype(np.float32), jnp.bfloat16)


def regroup_in(x_ref, matrix, rows):
    fields = x_ref.shape[1]
    height = fields * 32
    for half in range(2):
        tiles = [
            x_ref[0, :, :, 128 * (half + 2 * m) : 128 * (half + 2 * m) + 128].reshape(height, 128)
            for m in range(4)
        ]
        moved = jnp.dot(
            jnp.concatenate(tiles, axis=1), matrix[...], preferred_element_type=jnp.float32
        )
        for g in range(4):
            at = (half * 4 + g) * height
            rows[at : at + height, :] = moved[:, 128 * g : 128 * g + 128]


def plane_rows(fields, f, ii, jj):
    return pl.ds(jj * fields * 32 + f * 32 + ii, 8, stride=4)


def pack_kernel(
    sel_ref, x_ref, matrix, pick_z, pick_y, out_ref, faces, rows, edges
):
    step = pl.program_id(0)
    fields = x_ref.shape[1]
    height = fields * 32
    group = lane_iota() // 32
    regroup_in(x_ref, matrix, rows)
    along_z = jnp.dot(
        x_ref[0].reshape(height, 1024), pick_z[...], preferred_element_type=jnp.float32
    )
    ends = jnp.concatenate([x_ref[0, :, :, :128], x_ref[0, :, :, 896:]], axis=2)
    along_y = jnp.dot(
        ends.reshape(height, 256), pick_y[...], preferred_element_type=jnp.float32
    )
    for side in range(2):
        edges[side] = along_y[:, 128 * side : 128 * side + 128]
        edges[2 + side] = along_z[:, 128 * side : 128 * side + 128]

    for fp in range(fields // 2):
        got = [[], [], [], [], [], []]
        for f in (fp * 2, fp * 2 + 1):
            got[0].append(rows[pl.ds(f * 32, 8, stride=height), :])
            got[1].append(rows[pl.ds(f * 32 + 31, 8, stride=height), :])
            for face in range(2, 6):
                v = edges[face - 2, pl.ds(f * 32, 8, stride=4), :]
                for ii in range(1, 4):
                    part = edges[face - 2, pl.ds(f * 32 + ii, 8, stride=4), :]
                    v = jnp.where(group == ii, part, v)
                got[face].append(v)
        for face in range(6):
            both = jnp.concatenate(got[face], axis=0).astype(jnp.bfloat16)
            faces[step * 6 + face, fp * 16 : fp * 16 + 16, :] = both

    @pl.when(step == pl.num_programs(0) - 1)
    def _():
        def place(n, carry):
            out_ref[n] = faces[sel_ref[n]]
            return carry

        lax.fori_loop(0, out_ref.shape[0], place, 0, unroll=4)


def pack_faces(blocks, sel):
    per_dev, fields, cells, plane = blocks.shape
    return pl.pallas_call(
        pack_kernel,
        grid_spec=pltpu.PrefetchScalarGridSpec(
            num_scalar_prefetch=1,
            grid=(per_dev,),
            in_specs=[
                pl.BlockSpec((1, fields, cells, plane), lambda g, *_: (g, 0, 0, 0)),
                pl.BlockSpec((512, 512), lambda g, *_: (0, 0)),
                pl.BlockSpec((1024, 256), lambda g, *_: (0, 0)),
                pl.BlockSpec((256, 256), lambda g, *_: (0, 0)),
            ],
            out_specs=pl.BlockSpec((sel.shape[0], fields * 8, 128), lambda g, *_: (0, 0, 0)),
            scratch_shapes=[
                pltpu.VMEM((per_dev * 6, fields * 8, 128), jnp.bfloat16),
                pltpu.VMEM((fields * 256, 128), jnp.float32),
                pltpu.VMEM((4, fields * 32, 128), jnp.float32),
            ],
        ),
        out_shape=jax.ShapeDtypeStruct((sel.shape[0], fields * 8, 128), jnp.bfloat16),
        compiler_params=pltpu.CompilerParams(vmem_limit_bytes=VMEM_LIMIT),
    )(sel, blocks, regroup_matrix(), face_matrix_z(), face_matrix_y())


def advance_kernel(
    meta_ref, speed_ref, rate_ref, react_ref,
    x_ref, faces_ref, matrix, shift, spread_ends, coarse, o_ref,
    u, ghost, layers, ends, coef, rows, end_rows,
):
    fields = x_ref.shape[1]
    step = pl.program_id(0)
    count = pl.num_programs(0)
    per_dev = speed_ref.shape[0] // 3
    requests = per_dev * 6
    block = meta_ref[step]
    own_level = meta_ref[per_dev + block]
    substeps = jnp.left_shift(jnp.int32(1), own_level)
    scale = substeps.astype(jnp.float32)
    dt = jnp.where(own_level == 0, dt_base, jnp.where(own_level == 1, dt_base / 2, dt_base / 4))
    lane, row = lane_iota(), row_iota()
    regroup_in(x_ref, matrix, rows)

    tall_row = lax.broadcasted_iota(jnp.int32, (fields * 8, 128), 0)
    for face in range(6):
        request = block * 6 + face
        flag = meta_ref[2 * per_dev + requests + request]
        which = flag if face < 2 else flag * 2
        layer = faces_ref[meta_ref[2 * per_dev + request]]
        layers[face] = jnp.dot(layer, coarse[which], preferred_element_type=jnp.float32)
        if face < 2:

            @pl.when(flag > 0)
            def _():
                v = layers[face]
                size = fields * 8
                other = jnp.where(
                    tall_row % 2 == 0, pltpu.roll(v, size - 1, 0), pltpu.roll(v, 1, 0)
                )
                layers[face] = (v + other) * 0.5

    speeds = [speed_ref[block * 3 + d] for d in range(3)]
    minus = [jnp.maximum(v, 0.0) * scale * dt for v in speeds]
    plus = [-jnp.minimum(v, 0.0) * scale * dt for v in speeds]
    outflow = minus[0] + plus[0] + minus[1] + plus[1] + minus[2] + plus[2]

    def halo_low_x(plane, f, jj):
        edge = layers[0, pl.ds(f * 8 + jj, 1), :]
        return jnp.where(row == 0, edge, pltpu.roll(plane, 1, 0))

    def halo_high_x(plane, f, jj):
        edge = layers[1, pl.ds(f * 8 + jj, 1), :]
        return jnp.where(row == 7, edge, pltpu.roll(plane, 7, 0))

    def halo_low_y(plane, f, ii):
        return jnp.where(lane < 32, ends[0, f, ii], pltpu.roll(plane, 32, 1))

    def halo_high_y(plane, f, ii):
        return jnp.where(lane >= 96, ends[1, f, ii], pltpu.roll(plane, 96, 1))

    def prepare(f, carry):
        rate = rate_ref[f] * (scale * scale) * dt
        coef[f, 0] = jnp.full((8, 128), rate + minus[0])
        coef[f, 1] = jnp.full((8, 128), rate + plus[0])
        coef[f, 2] = jnp.full((8, 128), rate + minus[1])
        coef[f, 3] = jnp.full((8, 128), rate + plus[1])
        coef[f, 4] = jnp.full((8, 128), rate + minus[2])
        coef[f, 5] = jnp.full((8, 128), rate + plus[2])
        for e in range(fields):
            own = jnp.where(f == e, 1.0 - 6.0 * rate - outflow, 0.0)
            coef[f, 6 + e] = jnp.full((8, 128), dt * react_ref[f * fields + e] + own)

        at = pl.ds(pl.multiple_of(f * 8, 8), 8)
        low_y, high_y = layers[2, at, :], layers[3, at, :]
        low_z = layers[4, at, :] * (rate + minus[2])
        high_z = layers[5, at, :] * (rate + plus[2])
        for ii in range(4):
            here = lane // 32 == ii
            at = pl.ds(f * 32 + ii * 8, 8)
            end_rows[0, at, :] = jnp.where(here, low_z, 0.0)
            end_rows[1, at, :] = jnp.where(here, high_z, 0.0)
            ends[0, f, ii] = pltpu.roll(low_y, 128 - 32 * ii, 1) if ii else low_y
            ends[1, f, ii] = pltpu.roll(high_y, 96 - 32 * ii, 1) if ii != 3 else high_y
        for ii in range(4):
            for jj in range(8):
                plane = rows[plane_rows(fields, f, ii, jj), :]
                u[0, f, ii + 1, jj + 1] = plane
                if ii == 0:
                    u[0, f, 5, jj + 1] = halo_high_x(plane, f, jj)
                if ii == 3:
                    u[0, f, 0, jj + 1] = halo_low_x(plane, f, jj)
                if jj == 0:
                    u[0, f, ii + 1, 9] = halo_high_y(plane, f, ii)
                if jj == 7:
                    u[0, f, ii + 1, 0] = halo_low_y(plane, f, ii)
        return carry

    lax.fori_loop(0, fields, prepare, 0, unroll=2)

    low_high = jnp.concatenate([end_rows[0], end_rows[1]], axis=1)
    coarse_part = low_high.astype(jnp.bfloat16)
    fine_part = (low_high - coarse_part.astype(jnp.float32)).astype(jnp.bfloat16)
    spread = jnp.dot(
        jnp.concatenate([coarse_part, fine_part], axis=1),
        spread_ends[...],
        preferred_element_type=jnp.float32,
    )
    for jj in range(8):
        ghost[jj] = spread[:, 128 * jj : 128 * jj + 128]

    def substep(index, carry):
        now = index % 2
        later = 1 - now

        def planes(jj, inner):
            mid = [[u[now, f, ii + 1, jj + 1] for ii in range(4)] for f in range(fields)]
            value = jnp.concatenate([v for four in mid for v in four], axis=0)
            high = value.astype(jnp.bfloat16)
            low = (value - high.astype(jnp.float32)).astype(jnp.bfloat16)
            along_z = jnp.dot(
                jnp.concatenate([high, low], axis=1),
                shift[...],
                preferred_element_type=jnp.float32,
            )
            for f in range(fields):
                before = [u[now, f, 0, jj + 1]] + mid[f][:-1]
                after = mid[f][1:] + [u[now, f, 5, jj + 1]]
                total = []
                for ii in range(4):
                    at = f * 32 + ii * 8
                    v = ghost[jj, at : at + 8, :] + coef[f, 0] * before[ii]
                    v = v + coef[f, 1] * after[ii]
                    v = v + coef[f, 2] * u[now, f, ii + 1, jj]
                    v = v + coef[f, 3] * u[now, f, ii + 1, jj + 2]
                    v = v + coef[f, 4] * along_z[at : at + 8, :128]
                    v = v + coef[f, 5] * along_z[at : at + 8, 128:]
                    total.append(v)
                for e in range(fields):
                    weight = coef[f, 6 + e]
                    for ii in range(4):
                        total[ii] = total[ii] + weight * mid[e][ii]
                for ii in range(4):
                    u[later, f, ii + 1, jj + 1] = total[ii]
                u[later, f, 5, jj + 1] = halo_high_x(total[0], f, jj)
                u[later, f, 0, jj + 1] = halo_low_x(total[3], f, jj)
            return inner

        lax.fori_loop(0, 8, planes, 0)

        def halos(f, inner):
            for ii in range(4):
                u[later, f, ii + 1, 9] = halo_high_y(u[later, f, ii + 1, 1], f, ii)
                u[later, f, ii + 1, 0] = halo_low_y(u[later, f, ii + 1, 8], f, ii)
            return inner

        lax.fori_loop(0, fields, halos, 0, unroll=5)
        return carry

    lax.fori_loop(0, substeps, substep, 0)
    last = substeps % 2
    height = fields * 32

    def finish(f, carry):
        for ii in range(4):
            for jj in range(8):
                rows[plane_rows(fields, f, ii, jj), :] = u[last, f, ii + 1, jj + 1]
        return carry

    lax.fori_loop(0, fields, finish, 0)
    for half in range(2):
        tiles = []
        for g in range(4):
            at = (half * 4 + g) * height
            tiles.append(rows[at : at + height, :].astype(jnp.bfloat16))
        moved = jnp.dot(
            jnp.concatenate(tiles, axis=1), matrix[...], preferred_element_type=jnp.float32
        ).astype(jnp.bfloat16)
        for m in range(4):
            at = 128 * (half + 2 * m)
            o_ref[0, :, :, at : at + 128] = moved[:, 128 * m : 128 * m + 128].reshape(
                fields, 32, 128
            )


def advance(blocks, faces, meta, count, scalars, out_blocks):
    per_dev, fields, cells, plane = blocks.shape
    block_shape = (1, fields, cells, plane)
    picked = lambda g, meta, *_: (meta[g], 0, 0, 0)
    return pl.pallas_call(
        advance_kernel,
        grid_spec=pltpu.PrefetchScalarGridSpec(
            num_scalar_prefetch=4,
            grid=(count,),
            in_specs=[
                pl.BlockSpec(block_shape, picked),
                pl.BlockSpec(faces.shape, lambda g, *_: (0, 0, 0)),
                pl.BlockSpec((512, 512), lambda g, *_: (0, 0)),
                pl.BlockSpec((256, 256), lambda g, *_: (0, 0)),
                pl.BlockSpec((512, 1024), lambda g, *_: (0, 0)),
                pl.BlockSpec((3, 128, 128), lambda g, *_: (0, 0, 0)),
            ],
            out_specs=pl.BlockSpec(
                block_shape, picked if out_blocks > 1 else lambda g, *_: (0, 0, 0, 0)
            ),
            scratch_shapes=[
                pltpu.VMEM((2, fields, 6, 10, 8, 128), jnp.float32),
                pltpu.VMEM((8, fields * 32, 128), jnp.float32),
                pltpu.VMEM((6, fields * 8, 128), jnp.float32),
                pltpu.VMEM((2, fields, 4, 8, 128), jnp.float32),
                pltpu.VMEM((fields, 6 + fields, 8, 128), jnp.float32),
                pltpu.VMEM((fields * 256, 128), jnp.float32),
                pltpu.VMEM((2, fields * 32, 128), jnp.float32),
            ],
        ),
        out_shape=jax.ShapeDtypeStruct((out_blocks, fields, cells, plane), jnp.bfloat16),
        compiler_params=pltpu.CompilerParams(vmem_limit_bytes=VMEM_LIMIT),
        cost_estimate=pl.CostEstimate(
            flops=count * 40_000_000_000, bytes_accessed=count * 1_400_000, transcendentals=0
        ),
    )(
        meta, *scalars, blocks, faces,
        regroup_matrix(), shift_matrix(), end_matrix(), coarse_matrices(),
    )


def local(
    block_state,
    block_level,
    block_velocity,
    diffusivity,
    reaction_matrix,
    ghost_source,
    swap_bit,
    swap_slot,
):
    blocks = block_state[0]
    per_dev = blocks.shape[0]
    requests = per_dev * 6
    peers = lax.axis_size(("gy", "gz"))
    my_index = lax.axis_index(("gy", "gz"))
    base = my_index * per_dev
    wanted = ghost_source[0].reshape(peers, requests)
    order = jnp.arange(requests, dtype=jnp.int32)[None, :]
    code = order * 64 + wanted % per_dev * 6 + (order % 6 ^ 1)
    match = wanted // per_dev == my_index
    first = jnp.min(jnp.where(match, code, requests * 64), axis=1)
    final = jnp.max(jnp.where(match, code, 0), axis=1)
    sel = jnp.stack([first, final], axis=1).reshape(2 * peers) % 64

    outgoing = pack_faces(blocks, sel)
    arrived = lax.all_to_all(outgoing, ("gy", "gz"), split_axis=0, concat_axis=0, tiled=True)

    slot_here = swap_slot[0, 0, 0]
    bit_here = swap_bit[0, 0, 0]
    levels = block_level[0]
    mine = lax.dynamic_index_in_dim(wanted, my_index, 0, keepdims=False)
    source_dev = mine // per_dev
    earlier = jnp.arange(requests)[None, :] < jnp.arange(requests)[:, None]
    second = jnp.any((source_dev[:, None] == source_dev[None, :]) & earlier, axis=1)
    lookup = source_dev * 2 + second.astype(jnp.int32)
    own_levels = lax.dynamic_slice_in_dim(levels, base, per_dev, 0)
    numbers = jnp.arange(levels.shape[0], dtype=jnp.int32)
    donor_levels = jnp.sum(
        jnp.where(mine[:, None] == numbers[None, :], levels[None, :], 0), axis=1
    )
    differs = (donor_levels != jnp.repeat(own_levels, 6)).astype(jnp.int32)
    others = jnp.arange(per_dev, dtype=jnp.int32)
    others = (others + (others >= slot_here).astype(jnp.int32)) % per_dev
    tail = jnp.concatenate([own_levels, lookup, differs])
    meta_first = jnp.concatenate([jnp.full((per_dev,), slot_here), tail])
    meta_rest = jnp.concatenate([others, tail])
    scalars = (
        block_velocity[0].astype(jnp.float32).reshape(-1),
        diffusivity,
        reaction_matrix.reshape(-1),
    )
    departing = advance(blocks, arrived, meta_first, 1, scalars, 1)
    bit_count = lax.axis_size("gx").bit_length() - 1
    partners = [swapped(departing, "gx", bit_no) for bit_no in range(bit_count)]
    rest = advance(blocks, arrived, meta_rest, per_dev - 1, scalars, per_dev)
    coming = departing
    for bit_no in range(bit_count):
        coming = jnp.where(bit_here == bit_no, partners[bit_no], coming)
    result = lax.dynamic_update_index_in_dim(rest, coming[0], slot_here, 0)
    return result[None]


def solution(mesh):
    in_specs = (
        P("gx", ("gy", "gz"), None, None, None),
        P("gx", None),
        P("gx", ("gy", "gz"), None),
        P(),
        P(),
        P("gx", None, None),
        P("gx", "gy", "gz"),
        P("gx", "gy", "gz"),
    )
    out_specs = P("gx", ("gy", "gz"), None, None, None)
    return jax.shard_map(local, mesh=mesh, in_specs=in_specs, out_specs=out_specs, check_vma=False)
```

```python
import functools

import jax
import jax.numpy as jnp
import numpy as np
from jax import lax
from jax.experimental import pallas as pl
from jax.experimental.pallas import tpu as pltpu
from jax.sharding import PartitionSpec as P

dt_base = 0.05
VMEM_LIMIT = 56 * 1024 * 1024


def swapped(x, axis, bit):
    return lax.ppermute(x, axis, [(i, i ^ 1 << bit) for i in range(lax.axis_size(axis))])


def lane_iota():
    return lax.broadcasted_iota(jnp.int32, (8, 128), 1)


def row_iota():
    return lax.broadcasted_iota(jnp.int32, (8, 128), 0)


def ones_where(mask):
    return jnp.asarray(np.where(mask, 1.0, 0.0), jnp.bfloat16)


def regroup_matrix():
    r, c = np.arange(512)[:, None], np.arange(512)[None, :]
    return ones_where(c == r // 32 % 4 * 128 + r // 128 * 32 + r % 32)


def end_matrix():
    r, c = np.arange(512)[:, None], np.arange(1024)[None, :]
    side, j = r // 128 % 2, r % 32
    return ones_where((c // 128 + c // 32 % 4 * 8 == j) & (c % 32 == side * 31))


def face_matrix_z():
    r, c = np.arange(1024)[:, None], np.arange(256)[None, :]
    return ones_where((r // 32 == c % 32) & (r % 32 == c // 128 * 31))


def face_matrix_y():
    r, c = np.arange(256)[:, None], np.arange(256)[None, :]
    return ones_where((r // 32 == c // 128 * 7) & (r % 32 == c % 32))


def coarse_matrices():
    r, c = np.arange(128)[:, None], np.arange(128)[None, :]
    pairs = (r // 2 == c // 2) * 0.5
    patches = (r // 64 == c // 64) * (r % 32 // 2 == c % 32 // 2) * 0.25
    return jnp.asarray(np.stack([r == c, pairs, patches]).astype(np.float32), jnp.bfloat16)


def regroup_in(x_ref, matrix, rows):
    fields = x_ref.shape[1]
    height = fields * 32
    for half in range(2):
        tiles = [
            x_ref[0, :, :, 128 * (half + 2 * m) : 128 * (half + 2 * m) + 128].reshape(height, 128)
            for m in range(4)
        ]
        moved = jnp.dot(
            jnp.concatenate(tiles, axis=1), matrix[...], preferred_element_type=jnp.float32
        )
        for g in range(4):
            at = (half * 4 + g) * height
            rows[at : at + height, :] = moved[:, 128 * g : 128 * g + 128]


def plane_rows(fields, f, ii, jj):
    return pl.ds(jj * fields * 32 + f * 32 + ii, 8, stride=4)


def pack_kernel(
    sel_ref, x_ref, matrix, pick_z, pick_y, out_ref, faces, rows, edges
):
    step = pl.program_id(0)
    fields = x_ref.shape[1]
    height = fields * 32
    group = lane_iota() // 32
    regroup_in(x_ref, matrix, rows)
    along_z = jnp.dot(
        x_ref[0].reshape(height, 1024), pick_z[...], preferred_element_type=jnp.float32
    )
    ends = jnp.concatenate([x_ref[0, :, :, :128], x_ref[0, :, :, 896:]], axis=2)
    along_y = jnp.dot(
        ends.reshape(height, 256), pick_y[...], preferred_element_type=jnp.float32
    )
    for side in range(2):
        edges[side] = along_y[:, 128 * side : 128 * side + 128]
        edges[2 + side] = along_z[:, 128 * side : 128 * side + 128]

    for fp in range(fields // 2):
        got = [[], [], [], [], [], []]
        for f in (fp * 2, fp * 2 + 1):
            got[0].append(rows[pl.ds(f * 32, 8, stride=height), :])
            got[1].append(rows[pl.ds(f * 32 + 31, 8, stride=height), :])
            for face in range(2, 6):
                v = edges[face - 2, pl.ds(f * 32, 8, stride=4), :]
                for ii in range(1, 4):
                    part = edges[face - 2, pl.ds(f * 32 + ii, 8, stride=4), :]
                    v = jnp.where(group == ii, part, v)
                got[face].append(v)
        for face in range(6):
            both = jnp.concatenate(got[face], axis=0).astype(jnp.bfloat16)
            faces[step * 6 + face, fp * 16 : fp * 16 + 16, :] = both

    @pl.when(step == pl.num_programs(0) - 1)
    def _():
        def place(n, carry):
            out_ref[n] = faces[sel_ref[n]]
            return carry

        lax.fori_loop(0, out_ref.shape[0], place, 0, unroll=4)


def pack_faces(blocks, sel):
    per_dev, fields, cells, plane = blocks.shape
    return pl.pallas_call(
        pack_kernel,
        grid_spec=pltpu.PrefetchScalarGridSpec(
            num_scalar_prefetch=1,
            grid=(per_dev,),
            in_specs=[
                pl.BlockSpec((1, fields, cells, plane), lambda g, *_: (g, 0, 0, 0)),
                pl.BlockSpec((512, 512), lambda g, *_: (0, 0)),
                pl.BlockSpec((1024, 256), lambda g, *_: (0, 0)),
                pl.BlockSpec((256, 256), lambda g, *_: (0, 0)),
            ],
            out_specs=pl.BlockSpec((sel.shape[0], fields * 8, 128), lambda g, *_: (0, 0, 0)),
            scratch_shapes=[
                pltpu.VMEM((per_dev * 6, fields * 8, 128), jnp.bfloat16),
                pltpu.VMEM((fields * 256, 128), jnp.float32),
                pltpu.VMEM((4, fields * 32, 128), jnp.float32),
            ],
        ),
        out_shape=jax.ShapeDtypeStruct((sel.shape[0], fields * 8, 128), jnp.bfloat16),
        compiler_params=pltpu.CompilerParams(vmem_limit_bytes=VMEM_LIMIT),
    )(sel, blocks, regroup_matrix(), face_matrix_z(), face_matrix_y())


def step_terms(own_level, speed_ref, block):
    substeps = jnp.left_shift(jnp.int32(1), own_level)
    scale = substeps.astype(jnp.float32)
    dt = jnp.where(own_level == 0, dt_base, jnp.where(own_level == 1, dt_base / 2, dt_base / 4))
    speeds = [speed_ref[block * 3 + d] for d in range(3)]
    minus = [jnp.maximum(v, 0.0) * scale * dt for v in speeds]
    plus = [-jnp.minimum(v, 0.0) * scale * dt for v in speeds]
    return substeps, scale, dt, minus, plus


def fill_weights(coef, f, terms, rate_ref, react_ref, fields):
    _, scale, dt, minus, plus = terms
    k = lane_iota() % 32
    outflow = minus[0] + plus[0] + minus[1] + plus[1] + minus[2] + plus[2]
    rate = rate_ref[f] * (scale * scale) * dt
    coef[f, 0] = jnp.full((8, 128), rate + minus[0])
    coef[f, 1] = jnp.full((8, 128), rate + plus[0])
    coef[f, 2] = jnp.full((8, 128), rate + minus[1])
    coef[f, 3] = jnp.full((8, 128), rate + plus[1])
    coef[f, 4] = jnp.where(k == 0, 0.0, rate + minus[2])
    coef[f, 5] = jnp.where(k == 31, 0.0, rate + plus[2])
    for e in range(fields):
        own = jnp.where(f == e, 1.0 - 6.0 * rate - outflow, 0.0)
        coef[f, 6 + e] = jnp.full((8, 128), dt * react_ref[f * fields + e] + own)
    return rate


def update_planes(load, coef, jj, fields, ghost):
    mid = [[load(f, ii + 1, jj + 1) for ii in range(4)] for f in range(fields)]
    for f in range(fields):
        before = [load(f, 0, jj + 1)] + mid[f][:-1]
        after = mid[f][1:] + [load(f, 5, jj + 1)]
        total = []
        for ii in range(4):
            c = mid[f][ii]
            v = coef[f, 0] * before[ii]
            if ghost is not None:
                at = f * 32 + ii * 8
                v = v + ghost[jj, at : at + 8, :]
            v = v + coef[f, 1] * after[ii]
            v = v + coef[f, 2] * load(f, ii + 1, jj)
            v = v + coef[f, 3] * load(f, ii + 1, jj + 2)
            v = v + coef[f, 4] * pltpu.roll(c, 1, 1)
            v = v + coef[f, 5] * pltpu.roll(c, 127, 1)
            total.append(v)
        for e in range(fields):
            weight = coef[f, 6 + e]
            for ii in range(4):
                total[ii] = total[ii] + weight * mid[e][ii]
        yield f, total


def first_kernel(meta_ref, speed_ref, rate_ref, react_ref, x_ref, matrix, o_ref, u, coef, rows):
    fields = x_ref.shape[1]
    block = pl.program_id(0)
    per_dev = speed_ref.shape[0] // 3
    terms = step_terms(meta_ref[per_dev + block], speed_ref, block)
    lane, row = lane_iota(), row_iota()
    regroup_in(x_ref, matrix, rows)

    def prepare(f, carry):
        fill_weights(coef, f, terms, rate_ref, react_ref, fields)
        for ii in range(4):
            for jj in range(8):
                plane = rows[plane_rows(fields, f, ii, jj), :]
                u[f, ii + 1, jj + 1] = plane
                if ii == 0:
                    u[f, 5, jj + 1] = jnp.where(row == 7, 0.0, pltpu.roll(plane, 7, 0))
                if ii == 3:
                    u[f, 0, jj + 1] = jnp.where(row == 0, 0.0, pltpu.roll(plane, 1, 0))
                if jj == 0:
                    u[f, ii + 1, 9] = jnp.where(lane >= 96, 0.0, pltpu.roll(plane, 96, 1))
                if jj == 7:
                    u[f, ii + 1, 0] = jnp.where(lane < 32, 0.0, pltpu.roll(plane, 32, 1))
        return carry

    lax.fori_loop(0, fields, prepare, 0)

    def planes(jj, carry):
        load = lambda f, a, b: u[f, a, b]
        for f, total in update_planes(load, coef, jj, fields, None):
            for ii in range(4):
                o_ref[0, f, ii, jj] = total[ii]
        return carry

    lax.fori_loop(0, 8, planes, 0)


def advance_kernel(
    meta_ref, speed_ref, rate_ref, react_ref,
    x_ref, faces_ref, matrix, spread_ends, coarse, o_ref,
    u, ghost, layers, ends, coef, rows, end_rows,
):
    fields = x_ref.shape[1]
    step = pl.program_id(0)
    per_dev = speed_ref.shape[0] // 3
    requests = per_dev * 6
    block = meta_ref[step]
    own_level = meta_ref[per_dev + block]
    terms = step_terms(own_level, speed_ref, block)
    substeps, scale, dt, minus, plus = terms
    lane, row = lane_iota(), row_iota()

    tall_row = lax.broadcasted_iota(jnp.int32, (fields * 8, 128), 0)
    for face in range(6):
        request = block * 6 + face
        flag = meta_ref[2 * per_dev + requests + request]
        which = flag if face < 2 else flag * 2
        layer = faces_ref[meta_ref[2 * per_dev + request]]
        layers[face] = jnp.dot(layer, coarse[which], preferred_element_type=jnp.float32)
        if face < 2:

            @pl.when(flag > 0)
            def _():
                v = layers[face]
                size = fields * 8
                other = jnp.where(
                    tall_row % 2 == 0, pltpu.roll(v, size - 1, 0), pltpu.roll(v, 1, 0)
                )
                layers[face] = (v + other) * 0.5

    def halo_low_x(plane, f, jj):
        edge = layers[0, pl.ds(f * 8 + jj, 1), :]
        return jnp.where(row == 0, edge, pltpu.roll(plane, 1, 0))

    def halo_high_x(plane, f, jj):
        edge = layers[1, pl.ds(f * 8 + jj, 1), :]
        return jnp.where(row == 7, edge, pltpu.roll(plane, 7, 0))

    def halo_low_y(plane, f, ii):
        return jnp.where(lane < 32, ends[0, f, ii], pltpu.roll(plane, 32, 1))

    def halo_high_y(plane, f, ii):
        return jnp.where(lane >= 96, ends[1, f, ii], pltpu.roll(plane, 96, 1))

    def ghosts(f, carry):
        rate = fill_weights(coef, f, terms, rate_ref, react_ref, fields)
        at = pl.ds(pl.multiple_of(f * 8, 8), 8)
        low_y, high_y = layers[2, at, :], layers[3, at, :]
        low_z = layers[4, at, :] * (rate + minus[2])
        high_z = layers[5, at, :] * (rate + plus[2])
        for ii in range(4):
            here = lane // 32 == ii
            at = pl.ds(f * 32 + ii * 8, 8)
            end_rows[0, at, :] = jnp.where(here, low_z, 0.0)
            end_rows[1, at, :] = jnp.where(here, high_z, 0.0)
            ends[0, f, ii] = pltpu.roll(low_y, 128 - 32 * ii, 1) if ii else low_y
            ends[1, f, ii] = pltpu.roll(high_y, 96 - 32 * ii, 1) if ii != 3 else high_y
        return carry

    lax.fori_loop(0, fields, ghosts, 0, unroll=2)

    low_high = jnp.concatenate([end_rows[0], end_rows[1]], axis=1)
    coarse_part = low_high.astype(jnp.bfloat16)
    fine_part = (low_high - coarse_part.astype(jnp.float32)).astype(jnp.bfloat16)
    spread = jnp.dot(
        jnp.concatenate([coarse_part, fine_part], axis=1),
        spread_ends[...],
        preferred_element_type=jnp.float32,
    )
    for jj in range(8):
        ghost[jj] = spread[:, 128 * jj : 128 * jj + 128]

    def prepare(f, carry):
        for ii in range(4):
            for jj in range(8):
                plane = x_ref[0, f, ii, jj] + ghost[jj, pl.ds(f * 32 + ii * 8, 8), :]
                if ii == 0:
                    edge = layers[0, pl.ds(f * 8 + jj, 1), :]
                    plane = plane + jnp.where(row == 0, coef[f, 0] * edge, 0.0)
                if ii == 3:
                    edge = layers[1, pl.ds(f * 8 + jj, 1), :]
                    plane = plane + jnp.where(row == 7, coef[f, 1] * edge, 0.0)
                if jj == 0:
                    plane = plane + jnp.where(lane < 32, coef[f, 2] * ends[0, f, ii], 0.0)
                if jj == 7:
                    plane = plane + jnp.where(lane >= 96, coef[f, 3] * ends[1, f, ii], 0.0)
                u[1, f, ii + 1, jj + 1] = plane
                if ii == 0:
                    u[1, f, 5, jj + 1] = halo_high_x(plane, f, jj)
                if ii == 3:
                    u[1, f, 0, jj + 1] = halo_low_x(plane, f, jj)
                if jj == 0:
                    u[1, f, ii + 1, 9] = halo_high_y(plane, f, ii)
                if jj == 7:
                    u[1, f, ii + 1, 0] = halo_low_y(plane, f, ii)
        return carry

    lax.fori_loop(0, fields, prepare, 0, unroll=2)

    def substep(index, carry):
        now = index % 2
        later = 1 - now

        def planes(jj, inner):
            load = lambda f, a, b: u[now, f, a, b]
            for f, total in update_planes(load, coef, jj, fields, ghost):
                for ii in range(4):
                    u[later, f, ii + 1, jj + 1] = total[ii]
                u[later, f, 5, jj + 1] = halo_high_x(total[0], f, jj)
                u[later, f, 0, jj + 1] = halo_low_x(total[3], f, jj)
            return inner

        lax.fori_loop(0, 8, planes, 0)

        def halos(f, inner):
            for ii in range(4):
                u[later, f, ii + 1, 9] = halo_high_y(u[later, f, ii + 1, 1], f, ii)
                u[later, f, ii + 1, 0] = halo_low_y(u[later, f, ii + 1, 8], f, ii)
            return inner

        lax.fori_loop(0, fields, halos, 0, unroll=5)
        return carry

    lax.fori_loop(1, substeps, substep, 0)
    last = substeps % 2
    height = fields * 32

    def finish(f, carry):
        for ii in range(4):
            for jj in range(8):
                rows[plane_rows(fields, f, ii, jj), :] = u[last, f, ii + 1, jj + 1]
        return carry

    lax.fori_loop(0, fields, finish, 0)
    for half in range(2):
        tiles = []
        for g in range(4):
            at = (half * 4 + g) * height
            tiles.append(rows[at : at + height, :].astype(jnp.bfloat16))
        moved = jnp.dot(
            jnp.concatenate(tiles, axis=1), matrix[...], preferred_element_type=jnp.float32
        ).astype(jnp.bfloat16)
        for m in range(4):
            at = 128 * (half + 2 * m)
            o_ref[0, :, :, at : at + 128] = moved[:, 128 * m : 128 * m + 128].reshape(
                fields, 32, 128
            )


def start_blocks(blocks, meta, scalars):
    per_dev, fields, cells, plane = blocks.shape
    shape = (fields, 4, 8, 8, 128)
    return pl.pallas_call(
        first_kernel,
        grid_spec=pltpu.PrefetchScalarGridSpec(
            num_scalar_prefetch=4,
            grid=(per_dev,),
            in_specs=[
                pl.BlockSpec((1, fields, cells, plane), lambda g, *_: (g, 0, 0, 0)),
                pl.BlockSpec((512, 512), lambda g, *_: (0, 0)),
            ],
            out_specs=pl.BlockSpec((1,) + shape, lambda g, *_: (g, 0, 0, 0, 0, 0)),
            scratch_shapes=[
                pltpu.VMEM((fields, 6, 10, 8, 128), jnp.float32),
                pltpu.VMEM((fields, 6 + fields, 8, 128), jnp.float32),
                pltpu.VMEM((fields * 256, 128), jnp.float32),
            ],
        ),
        out_shape=jax.ShapeDtypeStruct((per_dev,) + shape, jnp.float32),
        compiler_params=pltpu.CompilerParams(vmem_limit_bytes=VMEM_LIMIT),
        cost_estimate=pl.CostEstimate(
            flops=20_000_000_000, bytes_accessed=8_000_000, transcendentals=0
        ),
    )(meta, *scalars, blocks, regroup_matrix())


def advance(started, faces, meta, count, scalars, out_blocks):
    fields = started.shape[1]
    cells, plane = 32, 1024
    block_shape = (1, fields, cells, plane)
    picked = lambda g, meta, *_: (meta[g], 0, 0, 0)
    return pl.pallas_call(
        advance_kernel,
        grid_spec=pltpu.PrefetchScalarGridSpec(
            num_scalar_prefetch=4,
            grid=(count,),
            in_specs=[
                pl.BlockSpec((1,) + started.shape[1:], lambda g, meta, *_: (meta[g], 0, 0, 0, 0, 0)),
                pl.BlockSpec(faces.shape, lambda g, *_: (0, 0, 0)),
                pl.BlockSpec((512, 512), lambda g, *_: (0, 0)),
                pl.BlockSpec((512, 1024), lambda g, *_: (0, 0)),
                pl.BlockSpec((3, 128, 128), lambda g, *_: (0, 0, 0)),
            ],
            out_specs=pl.BlockSpec(
                block_shape, picked if out_blocks > 1 else lambda g, *_: (0, 0, 0, 0)
            ),
            scratch_shapes=[
                pltpu.VMEM((2, fields, 6, 10, 8, 128), jnp.float32),
                pltpu.VMEM((8, fields * 32, 128), jnp.float32),
                pltpu.VMEM((6, fields * 8, 128), jnp.float32),
                pltpu.VMEM((2, fields, 4, 8, 128), jnp.float32),
                pltpu.VMEM((fields, 6 + fields, 8, 128), jnp.float32),
                pltpu.VMEM((fields * 256, 128), jnp.float32),
                pltpu.VMEM((2, fields * 32, 128), jnp.float32),
            ],
        ),
        out_shape=jax.ShapeDtypeStruct((out_blocks, fields, cells, plane), jnp.bfloat16),
        compiler_params=pltpu.CompilerParams(vmem_limit_bytes=VMEM_LIMIT),
        cost_estimate=pl.CostEstimate(
            flops=count * 40_000_000_000, bytes_accessed=count * 1_400_000, transcendentals=0
        ),
    )(
        meta, *scalars, started, faces,
        regroup_matrix(), end_matrix(), coarse_matrices(),
    )


def local(
    block_state,
    block_level,
    block_velocity,
    diffusivity,
    reaction_matrix,
    ghost_source,
    swap_bit,
    swap_slot,
):
    blocks = block_state[0]
    per_dev = blocks.shape[0]
    requests = per_dev * 6
    peers = lax.axis_size(("gy", "gz"))
    my_index = lax.axis_index(("gy", "gz"))
    base = my_index * per_dev
    wanted = ghost_source[0].reshape(peers, requests)
    order = jnp.arange(requests, dtype=jnp.int32)[None, :]
    code = order * 64 + wanted % per_dev * 6 + (order % 6 ^ 1)
    match = wanted // per_dev == my_index
    first = jnp.min(jnp.where(match, code, requests * 64), axis=1)
    final = jnp.max(jnp.where(match, code, 0), axis=1)
    sel = jnp.stack([first, final], axis=1).reshape(2 * peers) % 64

    outgoing = pack_faces(blocks, sel)
    arrived = lax.all_to_all(outgoing, ("gy", "gz"), split_axis=0, concat_axis=0, tiled=True)

    slot_here = swap_slot[0, 0, 0]
    bit_here = swap_bit[0, 0, 0]
    levels = block_level[0]
    mine = lax.dynamic_index_in_dim(wanted, my_index, 0, keepdims=False)
    source_dev = mine // per_dev
    earlier = jnp.arange(requests)[None, :] < jnp.arange(requests)[:, None]
    second = jnp.any((source_dev[:, None] == source_dev[None, :]) & earlier, axis=1)
    lookup = source_dev * 2 + second.astype(jnp.int32)
    own_levels = lax.dynamic_slice_in_dim(levels, base, per_dev, 0)
    numbers = jnp.arange(levels.shape[0], dtype=jnp.int32)
    donor_levels = jnp.sum(
        jnp.where(mine[:, None] == numbers[None, :], levels[None, :], 0), axis=1
    )
    differs = (donor_levels != jnp.repeat(own_levels, 6)).astype(jnp.int32)
    others = jnp.arange(per_dev, dtype=jnp.int32)
    others = (others + (others >= slot_here).astype(jnp.int32)) % per_dev
    tail = jnp.concatenate([own_levels, lookup, differs])
    meta_first = jnp.concatenate([jnp.full((per_dev,), slot_here), tail])
    meta_rest = jnp.concatenate([others, tail])
    scalars = (
        block_velocity[0].astype(jnp.float32).reshape(-1),
        diffusivity,
        reaction_matrix.reshape(-1),
    )
    started = start_blocks(blocks, meta_rest, scalars)
    departing = advance(started, arrived, meta_first, 1, scalars, 1)
    bit_count = lax.axis_size("gx").bit_length() - 1
    partners = [swapped(departing, "gx", bit_no) for bit_no in range(bit_count)]
    rest = advance(started, arrived, meta_rest, per_dev - 1, scalars, per_dev)
    coming = departing
    for bit_no in range(bit_count):
        coming = jnp.where(bit_here == bit_no, partners[bit_no], coming)
    result = lax.dynamic_update_index_in_dim(rest, coming[0], slot_here, 0)
    return result[None]


def solution(mesh):
    in_specs = (
        P("gx", ("gy", "gz"), None, None, None),
        P("gx", None),
        P("gx", ("gy", "gz"), None),
        P(),
        P(),
        P("gx", None, None),
        P("gx", "gy", "gz"),
        P("gx", "gy", "gz"),
    )
    out_specs = P("gx", ("gy", "gz"), None, None, None)
    return jax.shard_map(local, mesh=mesh, in_specs=in_specs, out_specs=out_specs, check_vma=False)
```

```python
import functools

import jax
import jax.numpy as jnp
import numpy as np
from jax import lax
from jax.experimental import pallas as pl
from jax.experimental.pallas import tpu as pltpu
from jax.sharding import PartitionSpec as P

dt_base = 0.05
VMEM_LIMIT = 56 * 1024 * 1024


def swapped(x, axis, bit):
    return lax.ppermute(x, axis, [(i, i ^ 1 << bit) for i in range(lax.axis_size(axis))])


def lane_iota():
    return lax.broadcasted_iota(jnp.int32, (8, 128), 1)


def row_iota():
    return lax.broadcasted_iota(jnp.int32, (8, 128), 0)


def ones_where(mask):
    return jnp.asarray(np.where(mask, 1.0, 0.0), jnp.bfloat16)


def regroup_matrix():
    r, c = np.arange(512)[:, None], np.arange(512)[None, :]
    return ones_where(c == r // 32 % 4 * 128 + r // 128 * 32 + r % 32)


def end_matrix():
    r, c = np.arange(256)[:, None], np.arange(1024)[None, :]
    side, j = r // 128, r % 32
    return ones_where((c // 128 + c // 32 % 4 * 8 == j) & (c % 32 == side * 31))


def face_matrix_z():
    r, c = np.arange(1024)[:, None], np.arange(256)[None, :]
    return ones_where((r // 32 == c % 32) & (r % 32 == c // 128 * 31))


def face_matrix_y():
    r, c = np.arange(256)[:, None], np.arange(256)[None, :]
    return ones_where((r // 32 == c // 128 * 7) & (r % 32 == c % 32))


def coarse_matrices():
    r, c = np.arange(128)[:, None], np.arange(128)[None, :]
    pairs = (r // 2 == c // 2) * 0.5
    patches = (r // 64 == c // 64) * (r % 32 // 2 == c % 32 // 2) * 0.25
    return jnp.asarray(np.stack([r == c, pairs, patches]).astype(np.float32), jnp.bfloat16)


def regroup_in(x_ref, matrix, rows):
    fields = x_ref.shape[1]
    height = fields * 32
    for half in range(2):
        tiles = [
            x_ref[0, :, :, 128 * (half + 2 * m) : 128 * (half + 2 * m) + 128].reshape(height, 128)
            for m in range(4)
        ]
        moved = jnp.dot(
            jnp.concatenate(tiles, axis=1), matrix[...], preferred_element_type=jnp.float32
        )
        for g in range(4):
            at = (half * 4 + g) * height
            rows[at : at + height, :] = moved[:, 128 * g : 128 * g + 128]


def plane_rows(fields, f, ii, jj):
    return pl.ds(jj * fields * 32 + f * 32 + ii, 8, stride=4)


def pack_kernel(
    sel_ref, x_ref, matrix, pick_z, pick_y, out_ref, faces, rows, edges
):
    step = pl.program_id(0)
    fields = x_ref.shape[1]
    height = fields * 32
    group = lane_iota() // 32
    regroup_in(x_ref, matrix, rows)
    along_z = jnp.dot(
        x_ref[0].reshape(height, 1024), pick_z[...], preferred_element_type=jnp.float32
    )
    ends = jnp.concatenate([x_ref[0, :, :, :128], x_ref[0, :, :, 896:]], axis=2)
    along_y = jnp.dot(
        ends.reshape(height, 256), pick_y[...], preferred_element_type=jnp.float32
    )
    for side in range(2):
        edges[side] = along_y[:, 128 * side : 128 * side + 128]
        edges[2 + side] = along_z[:, 128 * side : 128 * side + 128]

    for fp in range(fields // 2):
        got = [[], [], [], [], [], []]
        for f in (fp * 2, fp * 2 + 1):
            got[0].append(rows[pl.ds(f * 32, 8, stride=height), :])
            got[1].append(rows[pl.ds(f * 32 + 31, 8, stride=height), :])
            for face in range(2, 6):
                v = edges[face - 2, pl.ds(f * 32, 8, stride=4), :]
                for ii in range(1, 4):
                    part = edges[face - 2, pl.ds(f * 32 + ii, 8, stride=4), :]
                    v = jnp.where(group == ii, part, v)
                got[face].append(v)
        for face in range(6):
            both = jnp.concatenate(got[face], axis=0).astype(jnp.bfloat16)
            faces[step * 6 + face, fp * 16 : fp * 16 + 16, :] = both

    @pl.when(step == pl.num_programs(0) - 1)
    def _():
        def place(n, carry):
            out_ref[n] = faces[sel_ref[n]]
            return carry

        lax.fori_loop(0, out_ref.shape[0], place, 0, unroll=4)


def pack_faces(blocks, sel):
    per_dev, fields, cells, plane = blocks.shape
    return pl.pallas_call(
        pack_kernel,
        grid_spec=pltpu.PrefetchScalarGridSpec(
            num_scalar_prefetch=1,
            grid=(per_dev,),
            in_specs=[
                pl.BlockSpec((1, fields, cells, plane), lambda g, *_: (g, 0, 0, 0)),
                pl.BlockSpec((512, 512), lambda g, *_: (0, 0)),
                pl.BlockSpec((1024, 256), lambda g, *_: (0, 0)),
                pl.BlockSpec((256, 256), lambda g, *_: (0, 0)),
            ],
            out_specs=pl.BlockSpec((sel.shape[0], fields * 8, 128), lambda g, *_: (0, 0, 0)),
            scratch_shapes=[
                pltpu.VMEM((per_dev * 6, fields * 8, 128), jnp.bfloat16),
                pltpu.VMEM((fields * 256, 128), jnp.float32),
                pltpu.VMEM((4, fields * 32, 128), jnp.float32),
            ],
        ),
        out_shape=jax.ShapeDtypeStruct((sel.shape[0], fields * 8, 128), jnp.bfloat16),
        compiler_params=pltpu.CompilerParams(vmem_limit_bytes=VMEM_LIMIT),
    )(sel, blocks, regroup_matrix(), face_matrix_z(), face_matrix_y())


def step_terms(own_level, speed_ref, block):
    substeps = jnp.left_shift(jnp.int32(1), own_level)
    scale = substeps.astype(jnp.float32)
    dt = jnp.where(own_level == 0, dt_base, jnp.where(own_level == 1, dt_base / 2, dt_base / 4))
    speeds = [speed_ref[block * 3 + d] for d in range(3)]
    minus = [jnp.maximum(v, 0.0) * scale * dt for v in speeds]
    plus = [-jnp.minimum(v, 0.0) * scale * dt for v in speeds]
    return substeps, scale, dt, minus, plus


def fill_weights(coef, f, terms, rate_ref, react_ref, fields):
    _, scale, dt, minus, plus = terms
    k = lane_iota() % 32
    outflow = minus[0] + plus[0] + minus[1] + plus[1] + minus[2] + plus[2]
    rate = rate_ref[f] * (scale * scale) * dt
    coef[f, 0] = jnp.full((8, 128), rate + minus[0])
    coef[f, 1] = jnp.full((8, 128), rate + plus[0])
    coef[f, 2] = jnp.full((8, 128), rate + minus[1])
    coef[f, 3] = jnp.full((8, 128), rate + plus[1])
    coef[f, 4] = jnp.where(k == 0, 0.0, rate + minus[2])
    coef[f, 5] = jnp.where(k == 31, 0.0, rate + plus[2])
    for e in range(fields):
        own = jnp.where(f == e, 1.0 - 6.0 * rate - outflow, 0.0)
        coef[f, 6 + e] = jnp.full((8, 128), dt * react_ref[f * fields + e] + own)
    return rate


def update_planes(load, coef, jj, fields, ghost, store):
    for first in (0, 2):
        pair = (first, first + 1)
        mid = [[load(f, ii + 1, jj + 1) for ii in pair] for f in range(fields)]
        for f in range(fields):
            before = [load(f, first, jj + 1), mid[f][0]]
            after = [mid[f][1], load(f, first + 3, jj + 1)]
            total = []
            for p, ii in enumerate(pair):
                c = mid[f][p]
                v = coef[f, 0] * before[p]
                if ghost is not None:
                    at = f * 32 + ii * 8
                    v = v + ghost[jj, at : at + 8, :]
                v = v + coef[f, 1] * after[p]
                v = v + coef[f, 2] * load(f, ii + 1, jj)
                v = v + coef[f, 3] * load(f, ii + 1, jj + 2)
                v = v + coef[f, 4] * pltpu.roll(c, 1, 1)
                v = v + coef[f, 5] * pltpu.roll(c, 127, 1)
                total.append(v)
            for e in range(fields):
                weight = coef[f, 6 + e]
                for p in range(2):
                    total[p] = total[p] + weight * mid[e][p]
            for p, ii in enumerate(pair):
                store(f, ii, total[p])


def first_kernel(meta_ref, speed_ref, rate_ref, react_ref, x_ref, matrix, o_ref, u, coef, rows):
    fields = x_ref.shape[1]
    block = pl.program_id(0)
    per_dev = speed_ref.shape[0] // 3
    terms = step_terms(meta_ref[per_dev + block], speed_ref, block)
    lane, row = lane_iota(), row_iota()
    regroup_in(x_ref, matrix, rows)

    def prepare(f, carry):
        fill_weights(coef, f, terms, rate_ref, react_ref, fields)
        for ii in range(4):
            for jj in range(8):
                plane = rows[plane_rows(fields, f, ii, jj), :]
                u[f, ii + 1, jj + 1] = plane
                if ii == 0:
                    u[f, 5, jj + 1] = jnp.where(row == 7, 0.0, pltpu.roll(plane, 7, 0))
                if ii == 3:
                    u[f, 0, jj + 1] = jnp.where(row == 0, 0.0, pltpu.roll(plane, 1, 0))
                if jj == 0:
                    u[f, ii + 1, 9] = jnp.where(lane >= 96, 0.0, pltpu.roll(plane, 96, 1))
                if jj == 7:
                    u[f, ii + 1, 0] = jnp.where(lane < 32, 0.0, pltpu.roll(plane, 32, 1))
        return carry

    lax.fori_loop(0, fields, prepare, 0)

    def planes(jj, carry):
        load = lambda f, a, b: u[f, a, b]

        def store(f, ii, value):
            o_ref[0, f, ii, jj] = value

        update_planes(load, coef, jj, fields, None, store)
        return carry

    lax.fori_loop(0, 8, planes, 0)


def advance_kernel(
    meta_ref, speed_ref, rate_ref, react_ref,
    x_ref, faces_ref, matrix, spread_ends, coarse, o_ref,
    u, ghost, layers, ends, coef, rows, end_rows,
):
    fields = x_ref.shape[1]
    step = pl.program_id(0)
    per_dev = speed_ref.shape[0] // 3
    requests = per_dev * 6
    block = meta_ref[step]
    own_level = meta_ref[per_dev + block]
    terms = step_terms(own_level, speed_ref, block)
    substeps, scale, dt, minus, plus = terms
    lane, row = lane_iota(), row_iota()

    tall_row = lax.broadcasted_iota(jnp.int32, (fields * 8, 128), 0)
    for face in range(6):
        request = block * 6 + face
        flag = meta_ref[2 * per_dev + requests + request]
        which = flag if face < 2 else flag * 2
        layer = faces_ref[meta_ref[2 * per_dev + request]]
        layers[face] = jnp.dot(layer, coarse[which], preferred_element_type=jnp.float32)
        if face < 2:

            @pl.when(flag > 0)
            def _():
                v = layers[face]
                size = fields * 8
                other = jnp.where(
                    tall_row % 2 == 0, pltpu.roll(v, size - 1, 0), pltpu.roll(v, 1, 0)
                )
                layers[face] = (v + other) * 0.5

    def halo_low_x(plane, f, jj):
        edge = layers[0, pl.ds(f * 8 + jj, 1), :]
        return jnp.where(row == 0, edge, pltpu.roll(plane, 1, 0))

    def halo_high_x(plane, f, jj):
        edge = layers[1, pl.ds(f * 8 + jj, 1), :]
        return jnp.where(row == 7, edge, pltpu.roll(plane, 7, 0))

    def halo_low_y(plane, f, ii):
        return jnp.where(lane < 32, ends[0, f, ii], pltpu.roll(plane, 32, 1))

    def halo_high_y(plane, f, ii):
        return jnp.where(lane >= 96, ends[1, f, ii], pltpu.roll(plane, 96, 1))

    def ghosts(f, carry):
        rate = fill_weights(coef, f, terms, rate_ref, react_ref, fields)
        at = pl.ds(pl.multiple_of(f * 8, 8), 8)
        low_y, high_y = layers[2, at, :], layers[3, at, :]
        low_z = layers[4, at, :] * (rate + minus[2])
        high_z = layers[5, at, :] * (rate + plus[2])
        for ii in range(4):
            here = lane // 32 == ii
            at = pl.ds(f * 32 + ii * 8, 8)
            end_rows[0, at, :] = jnp.where(here, low_z, 0.0)
            end_rows[1, at, :] = jnp.where(here, high_z, 0.0)
            ends[0, f, ii] = pltpu.roll(low_y, 128 - 32 * ii, 1) if ii else low_y
            ends[1, f, ii] = pltpu.roll(high_y, 96 - 32 * ii, 1) if ii != 3 else high_y
        return carry

    lax.fori_loop(0, fields, ghosts, 0, unroll=2)

    low_high = jnp.concatenate([end_rows[0], end_rows[1]], axis=1)
    coarse_part = low_high.astype(jnp.bfloat16)
    fine_part = (low_high - coarse_part.astype(jnp.float32)).astype(jnp.bfloat16)
    spread = jnp.dot(
        jnp.concatenate([coarse_part, fine_part], axis=0),
        spread_ends[...],
        preferred_element_type=jnp.float32,
    )
    for jj in range(8):
        both = spread[:, 128 * jj : 128 * jj + 128]
        ghost[jj] = both[: fields * 32] + both[fields * 32 :]

    def prepare(f, carry):
        for ii in range(4):
            for jj in range(8):
                plane = x_ref[0, f, ii, jj] + ghost[jj, pl.ds(f * 32 + ii * 8, 8), :]
                if ii == 0:
                    edge = layers[0, pl.ds(f * 8 + jj, 1), :]
                    plane = plane + jnp.where(row == 0, coef[f, 0] * edge, 0.0)
                if ii == 3:
                    edge = layers[1, pl.ds(f * 8 + jj, 1), :]
                    plane = plane + jnp.where(row == 7, coef[f, 1] * edge, 0.0)
                if jj == 0:
                    plane = plane + jnp.where(lane < 32, coef[f, 2] * ends[0, f, ii], 0.0)
                if jj == 7:
                    plane = plane + jnp.where(lane >= 96, coef[f, 3] * ends[1, f, ii], 0.0)
                u[1, f, ii + 1, jj + 1] = plane
                if ii == 0:
                    u[1, f, 5, jj + 1] = halo_high_x(plane, f, jj)
                if ii == 3:
                    u[1, f, 0, jj + 1] = halo_low_x(plane, f, jj)
                if jj == 0:
                    u[1, f, ii + 1, 9] = halo_high_y(plane, f, ii)
                if jj == 7:
                    u[1, f, ii + 1, 0] = halo_low_y(plane, f, ii)
        return carry

    lax.fori_loop(0, fields, prepare, 0, unroll=2)

    def substep(index, carry):
        now = index % 2
        later = 1 - now

        def planes(jj, inner):
            load = lambda f, a, b: u[now, f, a, b]

            def store(f, ii, value):
                u[later, f, ii + 1, jj + 1] = value
                if ii == 0:
                    u[later, f, 5, jj + 1] = halo_high_x(value, f, jj)
                if ii == 3:
                    u[later, f, 0, jj + 1] = halo_low_x(value, f, jj)

            update_planes(load, coef, jj, fields, ghost, store)
            return inner

        lax.fori_loop(0, 8, planes, 0)

        def halos(f, inner):
            for ii in range(4):
                u[later, f, ii + 1, 9] = halo_high_y(u[later, f, ii + 1, 1], f, ii)
                u[later, f, ii + 1, 0] = halo_low_y(u[later, f, ii + 1, 8], f, ii)
            return inner

        lax.fori_loop(0, fields, halos, 0, unroll=5)
        return carry

    lax.fori_loop(1, substeps, substep, 0)
    last = substeps % 2
    height = fields * 32

    def finish(f, carry):
        for ii in range(4):
            for jj in range(8):
                rows[plane_rows(fields, f, ii, jj), :] = u[last, f, ii + 1, jj + 1]
        return carry

    lax.fori_loop(0, fields, finish, 0)
    for half in range(2):
        tiles = []
        for g in range(4):
            at = (half * 4 + g) * height
            tiles.append(rows[at : at + height, :].astype(jnp.bfloat16))
        moved = jnp.dot(
            jnp.concatenate(tiles, axis=1), matrix[...], preferred_element_type=jnp.float32
        ).astype(jnp.bfloat16)
        for m in range(4):
            at = 128 * (half + 2 * m)
            o_ref[0, :, :, at : at + 128] = moved[:, 128 * m : 128 * m + 128].reshape(
                fields, 32, 128
            )


def start_blocks(blocks, meta, scalars):
    per_dev, fields, cells, plane = blocks.shape
    shape = (fields, 4, 8, 8, 128)
    return pl.pallas_call(
        first_kernel,
        grid_spec=pltpu.PrefetchScalarGridSpec(
            num_scalar_prefetch=4,
            grid=(per_dev,),
            in_specs=[
                pl.BlockSpec((1, fields, cells, plane), lambda g, *_: (g, 0, 0, 0)),
                pl.BlockSpec((512, 512), lambda g, *_: (0, 0)),
            ],
            out_specs=pl.BlockSpec((1,) + shape, lambda g, *_: (g, 0, 0, 0, 0, 0)),
            scratch_shapes=[
                pltpu.VMEM((fields, 6, 10, 8, 128), jnp.float32),
                pltpu.VMEM((fields, 6 + fields, 8, 128), jnp.float32),
                pltpu.VMEM((fields * 256, 128), jnp.float32),
            ],
        ),
        out_shape=jax.ShapeDtypeStruct((per_dev,) + shape, jnp.float32),
        compiler_params=pltpu.CompilerParams(vmem_limit_bytes=VMEM_LIMIT),
        cost_estimate=pl.CostEstimate(
            flops=20_000_000_000, bytes_accessed=8_000_000, transcendentals=0
        ),
    )(meta, *scalars, blocks, regroup_matrix())


def advance(started, faces, meta, count, scalars, out_blocks):
    fields = started.shape[1]
    cells, plane = 32, 1024
    block_shape = (1, fields, cells, plane)
    picked = lambda g, meta, *_: (meta[g], 0, 0, 0)
    return pl.pallas_call(
        advance_kernel,
        grid_spec=pltpu.PrefetchScalarGridSpec(
            num_scalar_prefetch=4,
            grid=(count,),
            in_specs=[
                pl.BlockSpec((1,) + started.shape[1:], lambda g, meta, *_: (meta[g], 0, 0, 0, 0, 0)),
                pl.BlockSpec(faces.shape, lambda g, *_: (0, 0, 0)),
                pl.BlockSpec((512, 512), lambda g, *_: (0, 0)),
                pl.BlockSpec((256, 1024), lambda g, *_: (0, 0)),
                pl.BlockSpec((3, 128, 128), lambda g, *_: (0, 0, 0)),
            ],
            out_specs=pl.BlockSpec(
                block_shape, picked if out_blocks > 1 else lambda g, *_: (0, 0, 0, 0)
            ),
            scratch_shapes=[
                pltpu.VMEM((2, fields, 6, 10, 8, 128), jnp.float32),
                pltpu.VMEM((8, fields * 32, 128), jnp.float32),
                pltpu.VMEM((6, fields * 8, 128), jnp.float32),
                pltpu.VMEM((2, fields, 4, 8, 128), jnp.float32),
                pltpu.VMEM((fields, 6 + fields, 8, 128), jnp.float32),
                pltpu.VMEM((fields * 256, 128), jnp.float32),
                pltpu.VMEM((2, fields * 32, 128), jnp.float32),
            ],
        ),
        out_shape=jax.ShapeDtypeStruct((out_blocks, fields, cells, plane), jnp.bfloat16),
        compiler_params=pltpu.CompilerParams(vmem_limit_bytes=VMEM_LIMIT),
        cost_estimate=pl.CostEstimate(
            flops=count * 40_000_000_000, bytes_accessed=count * 1_400_000, transcendentals=0
        ),
    )(
        meta, *scalars, started, faces,
        regroup_matrix(), end_matrix(), coarse_matrices(),
    )


def local(
    block_state,
    block_level,
    block_velocity,
    diffusivity,
    reaction_matrix,
    ghost_source,
    swap_bit,
    swap_slot,
):
    blocks = block_state[0]
    per_dev = blocks.shape[0]
    requests = per_dev * 6
    peers = lax.axis_size(("gy", "gz"))
    my_index = lax.axis_index(("gy", "gz"))
    base = my_index * per_dev
    wanted = ghost_source[0].reshape(peers, requests)
    order = jnp.arange(requests, dtype=jnp.int32)[None, :]
    code = order * 64 + wanted % per_dev * 6 + (order % 6 ^ 1)
    match = wanted // per_dev == my_index
    first = jnp.min(jnp.where(match, code, requests * 64), axis=1)
    final = jnp.max(jnp.where(match, code, 0), axis=1)
    sel = jnp.stack([first, final], axis=1).reshape(2 * peers) % 64

    outgoing = pack_faces(blocks, sel)
    arrived = lax.all_to_all(outgoing, ("gy", "gz"), split_axis=0, concat_axis=0, tiled=True)

    slot_here = swap_slot[0, 0, 0]
    bit_here = swap_bit[0, 0, 0]
    levels = block_level[0]
    mine = lax.dynamic_index_in_dim(wanted, my_index, 0, keepdims=False)
    source_dev = mine // per_dev
    earlier = jnp.arange(requests)[None, :] < jnp.arange(requests)[:, None]
    second = jnp.any((source_dev[:, None] == source_dev[None, :]) & earlier, axis=1)
    lookup = source_dev * 2 + second.astype(jnp.int32)
    own_levels = lax.dynamic_slice_in_dim(levels, base, per_dev, 0)
    numbers = jnp.arange(levels.shape[0], dtype=jnp.int32)
    donor_levels = jnp.sum(
        jnp.where(mine[:, None] == numbers[None, :], levels[None, :], 0), axis=1
    )
    differs = (donor_levels != jnp.repeat(own_levels, 6)).astype(jnp.int32)
    others = jnp.arange(per_dev, dtype=jnp.int32)
    others = (others + (others >= slot_here).astype(jnp.int32)) % per_dev
    tail = jnp.concatenate([own_levels, lookup, differs])
    meta_first = jnp.concatenate([jnp.full((per_dev,), slot_here), tail])
    meta_rest = jnp.concatenate([others, tail])
    scalars = (
        block_velocity[0].astype(jnp.float32).reshape(-1),
        diffusivity,
        reaction_matrix.reshape(-1),
    )
    started = start_blocks(blocks, meta_rest, scalars)
    departing = advance(started, arrived, meta_first, 1, scalars, 1)
    bit_count = lax.axis_size("gx").bit_length() - 1
    partners = [swapped(departing, "gx", bit_no) for bit_no in range(bit_count)]
    rest = advance(started, arrived, meta_rest, per_dev - 1, scalars, per_dev)
    coming = departing
    for bit_no in range(bit_count):
        coming = jnp.where(bit_here == bit_no, partners[bit_no], coming)
    result = lax.dynamic_update_index_in_dim(rest, coming[0], slot_here, 0)
    return result[None]


def solution(mesh):
    in_specs = (
        P("gx", ("gy", "gz"), None, None, None),
        P("gx", None),
        P("gx", ("gy", "gz"), None),
        P(),
        P(),
        P("gx", None, None),
        P("gx", "gy", "gz"),
        P("gx", "gy", "gz"),
    )
    out_specs = P("gx", ("gy", "gz"), None, None, None)
    return jax.shard_map(local, mesh=mesh, in_specs=in_specs, out_specs=out_specs, check_vma=False)
```
